128 devices in a mesh: side: 2 (over z_lo), grp: 32 (over x, y, core), tp: 2 (over z_hi).
Axes of the slice: x: 4, y: 4, z: 4 (z_hi: 2, z_lo: 2; z = z_hi * 2 + z_lo), core: 2. Of those that a mesh axis runs over, the one named last changes fastest.
Arguments:
- query: bfloat16 [2, 256, 8192], P(None, 'grp', ('side', 'tp'))
- cache: bfloat16 [2, 256, 2, 4, 1024, 128], P(None, 'grp', None, ('side', 'tp'))
- cache_len: int32 [2, 256], P(None, 'grp'), may hold values from 1 to 1024, 131072 in all within a row
- row_slot: int32 [2, 256], replicated, may hold values from 0 to 255, each once within a row
- resid: bfloat16 [2, 256, 8192], P(None, None, 'grp')
- w_out: bfloat16 [8192, 8192], P(('side', 'tp'), 'grp'), may hold values from -0.5 to 0.5
- norm_gain: float32 [8192], P('grp'), may hold values from 0.1 to 1.9
- w_gate_up: bfloat16 [8192, 2, 32768], P(None, None, ('side', 'grp', 'tp')), may hold values from -0.25 to 0.25
- w_down: bfloat16 [32768, 8192], P(('side', 'grp', 'tp')), may hold values from -0.125 to 0.125
Outputs:
- layer_out: bfloat16 [2, 256, 8192], P(None, 'grp', ('side', 'tp'))
The draws below stay inside these ranges and needn't reach their ends.
Inputs may be any that keep to these rules, and one draw needn't show every extreme that they name: `cache_len`: the lengths of one micro-batch sum to 131072, and one slot of each micro-batch holds exactly 1024. Each micro-batch's row_slot names every slot once.
All inputs are finite; a program needn't handle non-finite values. No bound on the sum of `cache_len` on one device may be relied on, other than what follows from the above.
Results may differ from the reference program's by a relative error of at most 0.0062.
Values may be sent and summed in bfloat16 or wider, within the bound.
A program may use at most 128 MiB of HBM per device.

```python
import math
import jax
import jax.numpy as jnp
import numpy as np
from jax import lax

D = 8192
H = 64
KVH = 4
HD = 128
FF = 32768
MB = 2
LEN = 1024
ROWS = 256


def draw_query(key, part):
    key = jax.random.fold_in(key, 1)
    values = jax.random.normal(key, (MB, ROWS, KVH, H // KVH, HD), jnp.float32)
    return values.reshape(MB, ROWS, H * HD).astype(jnp.bfloat16)


def draw_cache(key, part):
    key = jax.random.fold_in(key, 2)
    values = jax.random.normal(key, (MB, ROWS, 2, KVH, LEN, HD), jnp.float32)
    return values.astype(jnp.bfloat16)


def draw_resid(key, part):
    key = jax.random.fold_in(key, 3)
    column = jnp.arange(D, dtype=jnp.float32) / D
    values = jax.random.normal(key, (MB, ROWS, D), jnp.float32) * (3.0 ** column)[None, None, :]
    return values.astype(jnp.bfloat16)


def raised(drawn, rng, source, target, blocks, factor):
    def block_of(dim):
        return (jnp.arange(drawn.shape[dim]) // (drawn.shape[dim] // blocks)).reshape((-1,) + (1,) * (drawn.ndim - 1 - dim))

    first = jax.random.permutation(rng, blocks)[block_of(target)]
    other_side = (block_of(target) + blocks // 2) % blocks
    return jnp.where((block_of(source) == first) | (block_of(source) == other_side), factor * drawn, drawn)


def levels(key, shape, cuts, least, top_value):
    loudness = 1.0
    for axis_at, shards_of in cuts:
        steps = jax.random.uniform(jax.random.fold_in(jax.random.fold_in(key, 6), axis_at), (shards_of,), jnp.float32, least / len(cuts), top_value / len(cuts))
        loudness = loudness * jnp.repeat(jnp.exp(steps), shape[axis_at] // shards_of).reshape((-1,) + (1,) * (len(shape) - 1 - axis_at))
    return loudness


def profile(number_of, total, bound, lean):
    portions = [(1 << 20) // math.isqrt(standing ** lean) + 1 for standing in range(2, number_of + 1)]
    spare, holding = total - bound - (number_of - 1), [1] * (number_of - 1)
    while spare > 0:
        free = [i for i in range(number_of - 1) if holding[i] < bound]
        mass, left = sum([portions[i] for i in free]), spare
        for i in free:
            extra = min(bound - holding[i], max(1, left * portions[i] // mass), spare)
            holding[i] = holding[i] + extra
            spare = spare - extra
    return np.array([bound] + holding)


def ragged_sizes(own_key, number_of, total, bound, skew):
    if number_of == 2:
        one = jax.random.randint(own_key, (), max(1, total - bound), min(bound, total - 1) + 1)
        return jnp.stack([one, total - one])
    lengths = jnp.asarray(profile(number_of, total, bound, skew), jnp.int32)
    pairs = (number_of - 1) // 2
    giver, sink = lengths[1:1 + 2 * pairs:2], lengths[2:2 + 2 * pairs:2]
    margin = jnp.minimum(giver - 1, bound - sink)
    shifted = jax.random.randint(jax.random.fold_in(own_key, 1), (pairs,), 0, 1 << 20) % (margin + 1)
    lengths = lengths.at[1:1 + 2 * pairs:2].set(giver - shifted).at[2:2 + 2 * pairs:2].set(sink + shifted)
    return lengths[jax.random.permutation(jax.random.fold_in(own_key, 2), number_of)]


def scatter_about(key, dims, spread, bound, shards=(), kind=jnp.bfloat16):
    result = spread * jax.random.normal(key, dims, jnp.float32)
    if shards:
        result = result * levels(key, dims, shards, -0.22, 0.18)
    return jnp.clip(result, -bound, bound).astype(kind)


def noise_with(own_key, shape, spread, bound, cuts, heavy, kind=jnp.bfloat16):
    array = spread * jax.random.normal(own_key, shape, jnp.float32)
    if cuts:
        array = array * levels(own_key, shape, cuts, -0.22, 0.18)
    return jnp.clip(raised(array, jax.random.fold_in(own_key, 3), *heavy), -bound, bound).astype(kind)


def setup_inputs(seed: int = 0) -> dict:
    streams_of = jax.random.split(jax.random.key(seed), 10)
    return {
        "query": draw_query(jax.random.fold_in(streams_of[9], 71), 0),
        "cache": draw_cache(jax.random.fold_in(streams_of[9], 71), 0),
        "cache_len": jax.vmap(lambda own: ragged_sizes(own, ROWS, ROWS * LEN // 2, LEN, 2))(jax.random.split(streams_of[2], MB)).reshape((MB, ROWS)).astype(jnp.int32),
        "row_slot": jax.vmap(lambda own: jax.random.permutation(own, ROWS))(jax.random.split(streams_of[3], MB)).reshape((MB, ROWS)).astype(jnp.int32),
        "resid": draw_resid(jax.random.fold_in(streams_of[9], 71), 0),
        "w_out": scatter_about(streams_of[5], (H * HD, D), (H * HD // 64) ** -0.5, 0.5, ((0, 4), (1, 32))),
        "norm_gain": jnp.clip(1.0 + 0.18 * jax.random.normal(streams_of[6], (D,), jnp.float32), 0.1, 1.9),
        "w_gate_up": noise_with(streams_of[7], (D, 2, FF), D ** -0.5, 0.25, ((2, 128),), (0, 2, 128, 5.5)),
        "w_down": noise_with(streams_of[8], (FF, D), FF ** -0.5, 0.125, ((0, 128),), (0, 1, 128, 5.5)),
    }


def attend_slot(inputs):
    queries, cached_keys, cached_values, length = inputs
    kv_heads = cached_keys.shape[0]
    head_size = cached_keys.shape[2]
    query_groups = queries.shape[0] // (kv_heads * head_size)
    grouped = queries.reshape(kv_heads, query_groups, head_size).astype(jnp.float32)
    scores = jnp.einsum('kgd,kld->kgl', grouped, cached_keys.astype(jnp.float32)) * (1.0 / math.sqrt(head_size))
    valid_mask = jnp.arange(cached_keys.shape[1]) < length
    scores = jnp.where(valid_mask[None, None, :], scores, -jnp.inf)
    weights = jax.nn.softmax(scores, axis=-1).astype(jnp.bfloat16)
    weights = lax.optimization_barrier(weights)
    attended = jnp.einsum('kgl,kld->kgd', weights.astype(jnp.float32), cached_values.astype(jnp.float32))
    return attended.astype(jnp.bfloat16).reshape(-1)

def reference(query, cache, cache_len, row_slot, resid, w_out, norm_gain, w_gate_up, w_down):
    gate_flat = w_gate_up.reshape(D, 2 * FF)
    outputs = []
    for micro_index in range(MB):
        attended = lax.map(attend_slot, (query[micro_index], cache[micro_index, :, 0], cache[micro_index, :, 1], cache_len[micro_index]))
        projected = jnp.dot(attended, w_out, preferred_element_type=jnp.float32)
        mixed = resid[micro_index].astype(jnp.float32) + projected[row_slot[micro_index]]
        row_scale = lax.rsqrt(lax.optimization_barrier(jnp.mean(mixed * mixed, axis=1)) + 1e-05)
        normed = (mixed * row_scale[:, None] * norm_gain[None, :]).astype(jnp.bfloat16)
        gate_up = jnp.dot(normed, gate_flat, preferred_element_type=jnp.float32).reshape(ROWS, 2, FF)
        hidden = (jax.nn.silu(gate_up[:, 0]) * gate_up[:, 1]).astype(jnp.bfloat16)
        layer_rows = (mixed + jnp.dot(hidden, w_down, preferred_element_type=jnp.float32)).astype(jnp.bfloat16)
        outputs.append(layer_rows)
    return jnp.stack(outputs)
```

```python
import math

import jax
import jax.numpy as jnp
from jax import lax
from jax.experimental import pallas as pl
from jax.experimental.pallas import tpu as pltpu
from jax.sharding import PartitionSpec as P

MESH = pl.DeviceIdType.MESH
F32 = jnp.float32
BF16 = jnp.bfloat16
EPS = 1e-05
N = 4
COLS = (640, 640, 768)
STARTS = (0, 640, 1280)
GATHER_PARTS = ((0, 32, 0, 384), (32, 32, 0, 384), (0, 64, 384, 128))
ORDERS = ((0, 1, 2), (1, 2, 0), (2, 0, 1))
W_CHUNKS = 8


def column_shard(z):
    return lax.rem(z, 2) * 2 + z // 2


def static_column_shard(z):
    return (z % 2) * 2 + z // 2


def dot(a, b):
    return jnp.dot(a, b, preferred_element_type=F32)


def layer_kernel(
    att_ref, rows_ref, owned_ref, resid_ref, wo_ref, gain_ref, wg_ref, wd_ref,
    out_ref,
    att_all, wo_all, resid_all, gain_all, w_raw, w_all, wd_all,
    proj_send, proj_recv, gathered, stats, acc, hid, pick, pick_sib,
    sums0, sums1, sums2, in10, in11, in12, t10, t11, t12,
    in20, in21, in22, t20, t21, t22, in30, in31, in32,
    res_own, res_send, res_recv,
    local_sem, sib_send, sib_recv, a_send, a_recv, b_send, b_recv,
    g_send, g_recv, s_send, s_recv, r_send, r_recv,
):
    g = lax.axis_index("grp")
    side = lax.axis_index("side")
    tp = lax.axis_index("tp")
    core = lax.rem(g, 2)
    y = lax.rem(g // 2, N)
    x = g // 8
    z = tp * 2 + side
    here = (x, y, z)
    xy = x * N + y

    def device(cx, cy, cz, cc):
        return {"side": lax.rem(cz, 2), "grp": (cx * N + cy) * 2 + cc, "tp": cz // 2}

    def along(axis, k):
        moved = list(here)
        moved[axis] = lax.rem(here[axis] + k, N)
        return moved[axis], device(moved[0], moved[1], moved[2], core)

    sibling = device(x, y, z, 1 - core)

    def remote(src, dst, send, recv, target):
        copy = pltpu.make_async_remote_copy(
            src_ref=src, dst_ref=dst, send_sem=send, recv_sem=recv,
            device_id=target, device_id_type=MESH,
        )
        copy.start()
        return copy

    def local(src, dst, sem):
        copy = pltpu.make_async_copy(src, dst, sem)
        copy.start()
        return copy

    barrier = pltpu.get_barrier_semaphore()
    for axis in range(3):
        for k in (1, 2, 3):
            pl.semaphore_signal(barrier, inc=1, device_id=along(axis, k)[1], device_id_type=MESH)
    pl.semaphore_signal(barrier, inc=1, device_id=sibling, device_id_type=MESH)
    raw_rows = w_raw.shape[0] // W_CHUNKS
    raw_loads = [
        local(wg_ref.at[pl.ds(i * raw_rows, raw_rows)], w_raw.at[pl.ds(i * raw_rows, raw_rows)], local_sem.at[i])
        for i in range(W_CHUNKS)
    ]
    own_loads = [
        local(wo_ref, wo_all.at[core], local_sem.at[W_CHUNKS]),
        local(resid_ref, resid_all.at[core], local_sem.at[W_CHUNKS + 1]),
        local(wd_ref, wd_all.at[core], local_sem.at[W_CHUNKS + 2]),
    ]
    att_all[x, y] = att_ref[...]
    gain_all[core] = gain_ref[...]
    pl.semaphore_wait(barrier, 10)

    half = att_all.shape[3] // 2
    first = []
    for part, axis in ((0, 0), (1, 1)):
        cols = pl.ds(part * half, half)
        for k in (1, 2, 3):
            ref = att_all.at[x, y, :, cols]
            first.append(remote(ref, ref, a_send.at[0, part, k - 1], a_recv.at[0, part, k - 1], along(axis, k)[1]))
    exchange = [
        remote(wo_ref, wo_all.at[core], sib_send.at[0], sib_recv.at[0], sibling),
        remote(resid_ref, resid_all.at[core], sib_send.at[1], sib_recv.at[1], sibling),
        remote(gain_ref, gain_all.at[core], sib_send.at[2], sib_recv.at[2], sibling),
        remote(wd_ref, wd_all.at[core], sib_send.at[3], sib_recv.at[3], sibling),
    ]

    p_out = lax.broadcasted_iota(jnp.int32, (256, 256), 0)
    p_in = lax.broadcasted_iota(jnp.int32, (256, 256), 1)
    order = jnp.where(p_in == (p_out % 64) * 4 + p_out // 64, 1.0, 0.0).astype(BF16)

    def untangle(chunk):
        raw_loads[chunk].wait()
        span = w_raw.shape[0] // (W_CHUNKS * 512)

        def step(u, _):
            unit = chunk * span + u
            row = pl.multiple_of(unit * 512, 512)
            both = jnp.concatenate([w_raw[pl.ds(row, 256)], w_raw[pl.ds(row + 256, 256)]], axis=1)
            apart = dot(order, both).astype(BF16)
            base = pl.multiple_of(unit * 128, 128)
            for l in range(2):
                for c in range(2):
                    rows = slice((l * 2 + c) * 64, (l * 2 + c) * 64 + 64)
                    lanes = pl.ds(c * 256 + l * 128, 128)
                    w_all[core, pl.ds(base, 64), lanes] = apart[rows, 0:128]
                    w_all[core, pl.ds(base + 64, 64), lanes] = apart[rows, 128:256]
            return 0

        lax.fori_loop(0, span, step, 0)
        block = w_all.at[core, pl.ds(chunk * span * 128, span * 128)]
        exchange.append(remote(block, block, sib_send.at[4 + chunk], sib_recv.at[4 + chunk], sibling))

    def slot_of(r, parity):
        return ((r // 16) * 2 + parity) * 8 + r % 8

    def choose(parity_slots, parity_rows):
        r = lax.broadcasted_iota(jnp.int32, (256, 256), 0)
        o = lax.broadcasted_iota(jnp.int32, (256, 256), 1)
        same = (r % 16) // 8 == (o % 16) // 8
        hit = same & (slot_of(r, parity_slots) == owned_ref[pl.ds(parity_rows, 1), :])
        return jnp.transpose(jnp.where(hit, 1.0, 0.0)).astype(BF16)

    for chunk in range(0, 3):
        untangle(chunk)
    for copy in first:
        copy.wait_recv()
    second = []
    for part, axis in ((0, 1), (1, 0)):
        cols = pl.ds(part * half, half)
        for k in (1, 2, 3):
            ref = att_all.at[:, y, :, cols] if part == 0 else att_all.at[x, :, :, cols]
            second.append(remote(ref, ref, a_send.at[1, part, k - 1], a_recv.at[1, part, k - 1], along(axis, k)[1]))
    for chunk in range(3, W_CHUNKS):
        untangle(chunk)
    own_loads[0].wait()
    exchange[0].wait_recv()
    for copy in second:
        copy.wait_recv()

    rows_all = att_all[...].reshape(256, 2 * half)
    for c in range(2):
        proj_send[:, :, c * 256:(c + 1) * 256] = dot(rows_all, wo_all[c]).astype(BF16).reshape(N, 64, 256)
    sends = []
    for k in (1, 2, 3):
        there, target = along(2, k)
        sends.append(remote(proj_send.at[there], proj_recv.at[k - 1], b_send.at[k - 1], b_recv.at[k - 1], target))

    own_loads[1].wait()
    exchange[1].wait_recv()
    exchange[2].wait_recv()
    r = z * 64 + lax.broadcasted_iota(jnp.int32, (64, 512), 0)
    o = lax.broadcasted_iota(jnp.int32, (64, 512), 1)
    hit = ((r % 16) // 8 == o // 256) & (slot_of(r, core) == rows_ref[...])
    served = jnp.where(hit, 1.0, 0.0).astype(BF16)
    resid_rows = jnp.concatenate([dot(served, resid_all[0]), dot(served, resid_all[1])], axis=1)
    gain_row = jnp.concatenate(
        [gain_all[0, 0:1], gain_all[0, 1:2], gain_all[1, 0:1], gain_all[1, 1:2]], axis=1
    )
    for copy in sends:
        copy.wait_recv()
    mixed = resid_rows + (
        (proj_send[z].astype(F32) + proj_recv[0].astype(F32))
        + (proj_recv[1].astype(F32) + proj_recv[2].astype(F32))
    )
    gathered[x, y, z] = (mixed * gain_row).astype(BF16)
    squares = jnp.sum(mixed * mixed, axis=1, keepdims=True)
    tall = jnp.concatenate([jnp.broadcast_to(squares, (64, 128)), jnp.zeros((64, 128), F32)], axis=0)
    stats[x, y, z, 0:4] = jnp.transpose(tall)[0:4]
    stats[x, y, z, 4:6] = gain_all[0, 0:2]
    stats[x, y, z, 6:8] = gain_all[1, 0:2]

    def gather_phase(phase):
        started = []
        for part, (row, rows, col, cols) in enumerate(GATHER_PARTS):
            axes = ORDERS[part]
            index = list(here)
            for done in axes[:phase]:
                index[done] = slice(None)
            block = gathered.at[index[0], index[1], index[2], pl.ds(row, rows), pl.ds(col, cols)]
            for k in (1, 2, 3):
                target = along(axes[phase], k)[1]
                started.append(remote(block, block, g_send.at[phase, part, k - 1], g_recv.at[phase, part, k - 1], target))
                if part == 2:
                    tile = stats.at[index[0], index[1], index[2]]
                    started.append(remote(tile, tile, s_send.at[phase, k - 1], s_recv.at[phase, k - 1], target))
        return started

    gathers = []
    for phase in range(3):
        now = gather_phase(phase)
        if phase == 0:
            for parity in range(2):
                pick[parity] = choose(parity, core)
            pick_sib[...] = choose(core, 1 - core)
        for copy in now:
            copy.wait_recv()
        gathers += now

    for chunk in range(W_CHUNKS):
        exchange[4 + chunk].wait_recv()
    acc[...] = jnp.zeros_like(acc)

    def multiply(i, _):
        block = gathered[i // N, lax.rem(i, N)].reshape(256, 512)
        row = pl.multiple_of(i * 512, 512)
        for p in range(2):
            acc[:, p * 512:(p + 1) * 512] += dot(block, w_all[p, pl.ds(row, 512), :])
        return 0

    lax.fori_loop(0, 16, multiply, 0)
    columns = []
    total = jnp.sum(stats[...].reshape(16, N, 8, 128), axis=0)
    for zz in range(N):
        spread = jnp.transpose(jnp.broadcast_to(total[zz, 0:1], (128, 128)))
        columns.append(spread[0:64])
    row_scale = lax.rsqrt(jnp.concatenate(columns, axis=0) * (1.0 / 8192) + EPS)
    row_scale = jnp.concatenate([row_scale, row_scale], axis=1)
    for p in range(2):
        gate = acc[:, p * 512:p * 512 + 256] * row_scale
        up = acc[:, p * 512 + 256:p * 512 + 512] * row_scale
        hid[core, :, p * 256:(p + 1) * 256] = (gate / (1.0 + jnp.exp(-gate)) * up).astype(BF16)
    hid_copy = remote(hid.at[core], hid.at[core], sib_send.at[12], sib_recv.at[12], sibling)
    own_loads[2].wait()
    exchange[3].wait_recv()

    shard = column_shard(z)
    mine = pick[core, pl.ds(pl.multiple_of(xy * 16, 16), 16), :]
    other = pick_sib[pl.ds(pl.multiple_of(xy * 16, 16), 16), :]
    for j in range(N):
        block = gathered[shard, j].reshape(256, 512)
        res_own[:, j * 512:(j + 1) * 512] = dot(mine, block)
        res_send[:, j * 512:(j + 1) * 512] = dot(other, block).astype(BF16)
    res_copy = remote(res_send, res_recv, sib_send.at[13], sib_recv.at[13], sibling)
    hid_copy.wait_recv()

    ours = (dot(pick[0], hid[0]) + dot(pick[1], hid[1])).astype(BF16)
    sums = (sums0, sums1, sums2)
    in1 = (in10, in11, in12)
    t1 = (t10, t11, t12)
    in2 = (in20, in21, in22)
    t2 = (t20, t21, t22)
    in3 = (in30, in31, in32)
    reduces = {}
    for part in range(3):
        for zz in range(N):
            lanes = pl.ds(static_column_shard(zz) * 2048 + STARTS[part], COLS[part])
            value = dot(ours[:, 0:256], wd_all[0, :, lanes]) + dot(ours[:, 256:512], wd_all[1, :, lanes])
            sums[part][:, :, zz] = value.astype(BF16).reshape(N, N, 16, COLS[part])
        axis = ORDERS[part][0]
        for k in (1, 2, 3):
            there, target = along(axis, k)
            index = [slice(None)] * 3
            index[axis] = there
            reduces[0, part, k] = remote(
                sums[part].at[index[0], index[1], index[2]], in1[part].at[k - 1],
                r_send.at[0, part, k - 1], r_recv.at[0, part, k - 1], target,
            )

    def add(own, incoming):
        return (own.astype(F32) + incoming[0].astype(F32)) + (incoming[1].astype(F32) + incoming[2].astype(F32))

    for part in range(3):
        for k in (1, 2, 3):
            reduces[0, part, k].wait_recv()
        axes = ORDERS[part]

        def fold(i, _, part=part, axes=axes):
            left = sorted(axes[1:])
            index = [None] * 3
            index[axes[0]] = here[axes[0]]
            index[left[0]] = i // N
            index[left[1]] = lax.rem(i, N)
            i0, i1 = i // N, lax.rem(i, N)
            own = sums[part][index[0], index[1], index[2]]
            t1[part][i0, i1] = add(own, [in1[part][q, i0, i1] for q in range(3)]).astype(BF16)
            return 0

        lax.fori_loop(0, 16, fold, 0)
        left = sorted(axes[1:])
        place = left.index(axes[1])
        for k in (1, 2, 3):
            there, target = along(axes[1], k)
            src = t1[part].at[there] if place == 0 else t1[part].at[:, there]
            reduces[1, part, k] = remote(
                src, in2[part].at[k - 1], r_send.at[1, part, k - 1], r_recv.at[1, part, k - 1], target
            )
    for part in range(3):
        for k in (1, 2, 3):
            reduces[1, part, k].wait_recv()
        axes = ORDERS[part]
        place = sorted(axes[1:]).index(axes[1])
        coord = here[axes[1]]
        for i in range(N):
            own = t1[part][coord, i] if place == 0 else t1[part][i, coord]
            t2[part][i] = add(own, [in2[part][q, i] for q in range(3)]).astype(BF16)
        for k in (1, 2, 3):
            there, target = along(axes[2], k)
            reduces[2, part, k] = remote(
                t2[part].at[there], in3[part].at[k - 1],
                r_send.at[2, part, k - 1], r_recv.at[2, part, k - 1], target,
            )
    res_copy.wait_recv()
    pieces = []
    for j in range(N):
        for q in range(4):
            pieces.append(stats[shard, j, z, 4 + q:5 + q])
    residual = (res_own[...] + res_recv[...].astype(F32)) / jnp.concatenate(pieces, axis=1)
    for part in range(3):
        for k in (1, 2, 3):
            reduces[2, part, k].wait_recv()
        own = t2[part][here[ORDERS[part][2]]]
        total = add(own, [in3[part][q] for q in range(3)])
        lanes = slice(STARTS[part], STARTS[part] + COLS[part])
        out_ref[:, lanes] = (residual[:, lanes] + total).astype(BF16)

    for copy in first + second + exchange + sends + gathers + [hid_copy, res_copy] + list(reduces.values()):
        copy.wait_send()


def attend(query, cache, cache_len):
    micro_count, slot_count = query.shape[0], query.shape[1]
    positions, head_size = cache.shape[4], cache.shape[5]
    heads = query.shape[2] // head_size
    position_ids = jnp.arange(positions)
    outputs = []
    for m in range(micro_count):
        queries = query[m].reshape(slot_count, 1, heads, head_size)
        scores = jnp.einsum("rkgd,rkld->rkgl", queries, cache[m, :, 0], preferred_element_type=F32)
        scores = scores * (1.0 / math.sqrt(head_size))
        live = position_ids[None, None, None, :] < cache_len[m][:, None, None, None]
        scores = jnp.where(live, scores, -jnp.inf)
        weights = jax.nn.softmax(scores, axis=-1).astype(BF16)
        attended = jnp.einsum("rkgl,rkld->rkgd", weights, cache[m, :, 1], preferred_element_type=F32)
        outputs.append(attended.astype(BF16).reshape(slot_count, heads * head_size))
    return jnp.concatenate(outputs, axis=0)


def shards(query, cache, cache_len, row_slot, resid, w_out, norm_gain, w_gate_up, w_down):
    attended = attend(query, cache, cache_len)
    rows = row_slot.reshape(1, 512)
    owned = row_slot.reshape(2, 16, 2, 8).transpose(2, 1, 0, 3).reshape(2, 256)
    gain = jnp.tile(norm_gain.reshape(2, 128), (4, 1))
    raw = w_gate_up.reshape(8192, 2, 2, 128).transpose(0, 2, 1, 3).reshape(32768, 128)
    vmem = pl.BlockSpec(memory_space=pltpu.VMEM)
    hbm = pl.BlockSpec(memory_space=pl.ANY)
    sem = pltpu.SemaphoreType.DMA
    scratch = [
        pltpu.VMEM((N, N, 16, 2048), BF16),
        pltpu.VMEM((2, 2048, 256), BF16),
        pltpu.VMEM((2, 512, 256), BF16),
        pltpu.VMEM((2, 8, 128), F32),
        pltpu.VMEM((32768, 128), BF16),
        pltpu.VMEM((2, 8192, 512), BF16),
        pltpu.VMEM((2, 256, 8192), BF16),
        pltpu.VMEM((N, 64, 512), BF16),
        pltpu.VMEM((3, 64, 512), BF16),
        pltpu.VMEM((N, N, N, 64, 512), BF16),
        pltpu.VMEM((N, N, N, 8, 128), F32),
        pltpu.VMEM((256, 1024), F32),
        pltpu.VMEM((2, 256, 512), BF16),
        pltpu.VMEM((2, 256, 256), BF16),
        pltpu.VMEM((256, 256), BF16),
    ]
    scratch += [pltpu.VMEM((N, N, N, 16, c), BF16) for c in COLS]
    scratch += [pltpu.VMEM((3, N, N, 16, c), BF16) for c in COLS]
    scratch += [pltpu.VMEM((N, N, 16, c), BF16) for c in COLS]
    scratch += [pltpu.VMEM((3, N, 16, c), BF16) for c in COLS]
    scratch += [pltpu.VMEM((N, 16, c), BF16) for c in COLS]
    scratch += [pltpu.VMEM((3, 16, c), BF16) for c in COLS]
    scratch += [
        pltpu.VMEM((16, 2048), F32),
        pltpu.VMEM((16, 2048), BF16),
        pltpu.VMEM((16, 2048), BF16),
    ]
    scratch += [
        sem((W_CHUNKS + 3,)),
        sem((14,)), sem((14,)),
        sem((2, 2, 3)), sem((2, 2, 3)),
        sem((3,)), sem((3,)),
        sem((3, 3, 3)), sem((3, 3, 3)),
        sem((3, 3)), sem((3, 3)),
        sem((3, 3, 3)), sem((3, 3, 3)),
    ]
    out = pl.pallas_call(
        layer_kernel,
        out_shape=jax.ShapeDtypeStruct((16, 2048), BF16),
        in_specs=[vmem, vmem, vmem, hbm, hbm, vmem, hbm, hbm],
        out_specs=vmem,
        scratch_shapes=scratch,
        compiler_params=pltpu.CompilerParams(
            collective_id=0, has_side_effects=True, vmem_limit_bytes=60 * 1024 * 1024
        ),
        name="layer",
    )(attended, rows, owned, resid.reshape(512, 256), w_out, gain, raw, w_down)
    return out.reshape(2, 8, 2048)


def solution(mesh):
    placed = (
        P(None, "grp", ("side", "tp")),
        P(None, "grp", None, ("side", "tp"), None, None),
        P(None, "grp"),
        P(),
        P(None, None, "grp"),
        P(("side", "tp"), "grp"),
        P("grp"),
        P(None, None, ("side", "grp", "tp")),
        P(("side", "grp", "tp"), None),
    )
    return jax.shard_map(
        shards,
        mesh=mesh,
        in_specs=placed,
        out_specs=P(None, "grp", ("side", "tp")),
        check_vma=False,
    )
```

```python
import math

import jax
import jax.numpy as jnp
from jax import lax
from jax.experimental import pallas as pl
from jax.experimental.pallas import tpu as pltpu
from jax.sharding import PartitionSpec as P

MESH = pl.DeviceIdType.MESH
F32 = jnp.float32
BF16 = jnp.bfloat16
EPS = 1e-05
N = 4
MICRO = 2
COLS = (384, 384, 256)
STARTS = (0, 384, 768)
GATHER_PARTS = ((0, 16, 0, 384), (16, 16, 0, 384), (0, 32, 384, 128))
ORDERS = ((0, 1, 2), (1, 2, 0), (2, 0, 1))
W_CHUNKS = 8
W_SLOTS = 3


def dot(a, b):
    return jnp.dot(a, b, preferred_element_type=F32)


def layer_kernel(
    len_ref, query_ref, cache_ref, rows_ref, resid_ref, wo_ref, gain_ref, wg_ref, wd_ref,
    out_ref,
    kv, att_all, wo_all, resid_all, gain_all, w_raw, w_all, wd_all,
    proj_send, proj_recv, gathered, stats, acc, hid, pick,
    sums0, sums1, sums2, in10, in11, in12, t10, t11, t12,
    in20, in21, in22, t20, t21, t22, in30, in31, in32,
    res_own, res_send, res_recv,
    local_sem, sib_send, sib_recv, a_send, a_recv, b_send, b_recv,
    g_send, g_recv, s_send, s_recv, r_send, r_recv,
):
    g = lax.axis_index("grp")
    side = lax.axis_index("side")
    tp = lax.axis_index("tp")
    core = lax.rem(g, 2)
    y = lax.rem(g // 2, N)
    x = g // 8
    z = tp * 2 + side
    here = (x, y, z)
    xy = x * N + y
    shard = side * 2 + tp

    def device(cx, cy, cz, cc):
        return {"side": lax.rem(cz, 2), "grp": (cx * N + cy) * 2 + cc, "tp": cz // 2}

    def along(axis, k):
        moved = list(here)
        moved[axis] = lax.rem(here[axis] + k, N)
        return moved[axis], device(moved[0], moved[1], moved[2], core)

    sibling = device(x, y, z, 1 - core)
    all_sends = []

    def remote(src, dst, send, recv, target):
        copy = pltpu.make_async_remote_copy(
            src_ref=src, dst_ref=dst, send_sem=send, recv_sem=recv,
            device_id=target, device_id_type=MESH,
        )
        copy.start()
        all_sends.append(copy)
        return copy

    def local(src, dst, sem):
        copy = pltpu.make_async_copy(src, dst, sem)
        copy.start()
        return copy

    def received(copies):
        for copy in copies:
            copy.wait_recv()

    barrier = pltpu.get_barrier_semaphore()
    for axis in range(3):
        for k in (1, 2, 3):
            pl.semaphore_signal(barrier, inc=1, device_id=along(axis, k)[1], device_id_type=MESH)
    pl.semaphore_signal(barrier, inc=1, device_id=sibling, device_id_type=MESH)

    kv_loads = [
        [local(cache_ref.at[m, :, i], kv.at[m, i], local_sem.at[m * 2 + i]) for i in range(2)]
        for m in range(MICRO)
    ]
    raw_rows = w_raw.shape[1]

    def load_raw(chunk):
        return local(
            wg_ref.at[pl.ds(chunk * raw_rows, raw_rows)], w_raw.at[chunk % W_SLOTS], local_sem.at[8 + chunk]
        )

    raw_loads = {chunk: load_raw(chunk) for chunk in range(W_SLOTS)}
    wo_load = local(wo_ref, wo_all.at[core], local_sem.at[4])
    resid_load = local(resid_ref, resid_all.at[core], local_sem.at[5])
    wd_load = local(wd_ref, wd_all.at[core], local_sem.at[6])

    def attend(m):
        queries = query_ref[m].astype(F32)
        heads = queries.shape[1] // 128
        stacked = jnp.concatenate([queries[:, h * 128:(h + 1) * 128] for h in range(heads)], axis=0).astype(BF16)
        slot_id = lax.broadcasted_iota(jnp.int32, (heads * 8, 1), 0) % 8
        live = jnp.zeros((heads * 8, 1), jnp.int32)
        for s in range(8):
            live = jnp.where(slot_id == s, len_ref[m, s], live)
        kv_loads[m][0].wait()
        scores = None
        for s in range(8):
            one = lax.dot_general(stacked, kv[m, 0, s], (((1,), (1,)), ((), ())), preferred_element_type=F32)
            scores = one if s == 0 else jnp.where(slot_id == s, one, scores)
        position = lax.broadcasted_iota(jnp.int32, scores.shape, 1)
        scores = jnp.where(position < live, scores * (1.0 / math.sqrt(128)), -jnp.inf)
        top = jnp.max(scores, axis=1, keepdims=True)
        raised = jnp.exp(scores - top)
        total = jnp.sum(raised, axis=1, keepdims=True)
        weights = (raised / total).astype(BF16)
        kv_loads[m][1].wait()
        mixed = None
        for s in range(8):
            one = dot(weights, kv[m, 1, s])
            mixed = one if s == 0 else jnp.where(slot_id == s, one, mixed)
        halves = []
        for half in range(2):
            tiles = [mixed[(half * 8 + h) * 8:(half * 8 + h) * 8 + 8] for h in range(8)]
            halves.append(jnp.concatenate(tiles, axis=1))
        att_all[m, x, y] = jnp.concatenate(halves, axis=0).astype(BF16)

    def attended_phase(m, phase):
        copies = []
        for part in range(2):
            cols = pl.ds(part * 512, 512)
            axis = part if phase == 0 else 1 - part
            index = [x, y]
            if phase == 1:
                index[part] = slice(None)
            ref = att_all.at[m, index[0], index[1], :, cols]
            for k in (1, 2, 3):
                copies.append(remote(
                    ref, ref, a_send.at[m, phase, part, k - 1], a_recv.at[m, phase, part, k - 1], along(axis, k)[1]
                ))
        return copies

    p_out = lax.broadcasted_iota(jnp.int32, (256, 256), 0)
    p_in = lax.broadcasted_iota(jnp.int32, (256, 256), 1)
    order = jnp.where(p_in == (p_out % 64) * 4 + p_out // 64, 1.0, 0.0).astype(BF16)
    weight_copies = {}

    def untangle(chunk):
        raw_loads[chunk].wait()
        span = raw_rows // 512
        slot = chunk % W_SLOTS

        def step(u, _):
            row = pl.multiple_of(u * 512, 512)
            both = jnp.concatenate([w_raw[slot, pl.ds(row, 256)], w_raw[slot, pl.ds(row + 256, 256)]], axis=1)
            apart = dot(order, both).astype(BF16)
            base = pl.multiple_of((chunk * span + u) * 128, 128)
            for l in range(2):
                for c in range(2):
                    rows = slice((l * 2 + c) * 64, (l * 2 + c) * 64 + 64)
                    lanes = pl.ds(c * 256 + l * 128, 128)
                    w_all[core, pl.ds(base, 64), lanes] = apart[rows, 0:128]
                    w_all[core, pl.ds(base + 64, 64), lanes] = apart[rows, 128:256]
            return 0

        lax.fori_loop(0, span, step, 0)
        if chunk + W_SLOTS < W_CHUNKS:
            raw_loads[chunk + W_SLOTS] = load_raw(chunk + W_SLOTS)
        block = w_all.at[core, pl.ds(chunk * span * 128, span * 128)]
        weight_copies[chunk] = remote(block, block, sib_send.at[4 + chunk], sib_recv.at[4 + chunk], sibling)

    def slot_of(r, parity):
        return ((r // 8) * 2 + parity) * 8 + r % 8

    def choose(m):
        r = lax.broadcasted_iota(jnp.int32, (128, 256), 0)
        for i, parity in enumerate((core, 1 - core)):
            hit = jnp.where(slot_of(r, parity) == rows_ref[m:m + 1, :], 1.0, 0.0)
            turned = jnp.concatenate([jnp.transpose(hit[:, 0:128]), jnp.transpose(hit[:, 128:256])], axis=0)
            turned = turned.reshape(16, 2, 8, 128)
            even, odd = turned[:, 0].reshape(128, 128), turned[:, 1].reshape(128, 128)
            pick[m, i] = jnp.where(core == 0, even, odd)
            if i == 0:
                pick[m, 2] = jnp.where(core == 0, odd, even)

    def project(m):
        blocks = att_all[m].astype(F32).reshape(16, 2, 8, 1024)
        rows = jnp.concatenate([blocks[:, 0].reshape(128, 1024), blocks[:, 1].reshape(128, 1024)], axis=1).astype(BF16)
        for c in range(2):
            proj_send[m, :, :, c * 256:(c + 1) * 256] = dot(rows, wo_all[c]).astype(BF16).reshape(N, 32, 256)
        copies = []
        for k in (1, 2, 3):
            there, target = along(2, k)
            copies.append(remote(
                proj_send.at[m, there], proj_recv.at[m, k - 1], b_send.at[m, k - 1], b_recv.at[m, k - 1], target
            ))
        return copies

    def residual_rows(m):
        r = z * 32 + lax.broadcasted_iota(jnp.int32, (32, 256), 0)
        served = jnp.where(slot_of(r, core) == rows_ref[m:m + 1, :], 1.0, 0.0).astype(BF16)
        return jnp.concatenate([dot(served, resid_all[c, m * 256:(m + 1) * 256]) for c in range(2)], axis=1)

    def mix(m, resid_rows, gain_row):
        mixed = resid_rows + (
            (proj_send[m, z].astype(F32) + proj_recv[m, 0].astype(F32))
            + (proj_recv[m, 1].astype(F32) + proj_recv[m, 2].astype(F32))
        )
        gathered[m, x, y, z] = (mixed * gain_row).astype(BF16)
        squares = jnp.sum(mixed * mixed, axis=1, keepdims=True)
        tall = jnp.concatenate([jnp.broadcast_to(squares, (32, 128)), jnp.zeros((96, 128), F32)], axis=0)
        stats[m, x, y, z, 0:4] = jnp.transpose(tall)[0:4]
        stats[m, x, y, z, 4:6] = gain_all[0, 0:2]
        stats[m, x, y, z, 6:8] = gain_all[1, 0:2]

    def gather_phase(m, phase):
        copies = []
        for part, (row, rows, col, cols) in enumerate(GATHER_PARTS):
            axes = ORDERS[part]
            index = list(here)
            for done in axes[:phase]:
                index[done] = slice(None)
            block = gathered.at[m, index[0], index[1], index[2], pl.ds(row, rows), pl.ds(col, cols)]
            for k in (1, 2, 3):
                target = along(axes[phase], k)[1]
                copies.append(remote(
                    block, block, g_send.at[m, phase, part, k - 1], g_recv.at[m, phase, part, k - 1], target
                ))
                if part == 2:
                    tile = stats.at[m, index[0], index[1], index[2]]
                    copies.append(remote(
                        tile, tile, s_send.at[m, phase, k - 1], s_recv.at[m, phase, k - 1], target
                    ))
        return copies

    def feed(m):
        def multiply(i, _):
            block = jnp.concatenate([gathered[m, i, j].reshape(128, 512) for j in range(N)], axis=1)
            row = pl.multiple_of(i * 2048, 2048)
            for p in range(2):
                acc[:, p * 512:(p + 1) * 512] += dot(block, w_all[p, pl.ds(row, 2048), :])
            return 0

        acc[...] = jnp.zeros_like(acc)
        lax.fori_loop(0, N, multiply, 0)
        total = jnp.sum(stats[m].reshape(16, N, 8, 128), axis=0)
        columns = []
        for zz in range(N):
            spread = jnp.transpose(jnp.broadcast_to(total[zz, 0:1], (128, 128)))
            columns.append(spread[0:32])
        row_scale = lax.rsqrt(jnp.concatenate(columns, axis=0) * (1.0 / 8192) + EPS)
        row_scale = jnp.concatenate([row_scale, row_scale], axis=1)
        for p in range(2):
            gate = acc[:, p * 512:p * 512 + 256] * row_scale
            up = acc[:, p * 512 + 256:p * 512 + 512] * row_scale
            hid[m, core, :, p * 256:(p + 1) * 256] = (gate / (1.0 + jnp.exp(-gate)) * up).astype(BF16)
        block = hid.at[m, core]
        return remote(block, block, sib_send.at[12 + m], sib_recv.at[12 + m], sibling)

    def residual(m):
        row = pl.multiple_of(xy * 8, 8)
        wanted = jnp.concatenate([pick[m, 0, pl.ds(row, 8), :], pick[m, 2, pl.ds(row, 8), :]], axis=0).astype(BF16)
        found = [dot(wanted, gathered[m, shard, j].reshape(128, 512)) for j in range(N)]
        found = jnp.concatenate(found, axis=1)
        res_own[m] = found[0:8]
        res_send[m] = jnp.concatenate([found[8:16, 0:1024], found[8:16, 1024:2048]], axis=0).astype(BF16)
        return remote(res_send.at[m], res_recv.at[m], sib_send.at[14 + m], sib_recv.at[14 + m], sibling)

    sums = (sums0, sums1, sums2)
    in1 = (in10, in11, in12)
    t1 = (t10, t11, t12)
    in2 = (in20, in21, in22)
    t2 = (t20, t21, t22)
    in3 = (in30, in31, in32)

    def down(m):
        other = jnp.where(core == 0, hid[m, 1].astype(F32), hid[m, 0].astype(F32)).astype(BF16)
        ours = dot(pick[m, 0].astype(BF16), hid[m, core]) + dot(pick[m, 1].astype(BF16), other)
        ours = ours.astype(BF16)
        copies = [[], [], []]
        for part in range(3):
            width = COLS[part]
            for zz in range(N):
                base = ((zz % 2) * 2 + zz // 2) * 2048 + STARTS[part]
                halves = []
                for half in range(2):
                    lanes = pl.ds(base + half * 1024, width)
                    value = dot(ours[:, 0:256], wd_all[0, :, lanes]) + dot(ours[:, 256:512], wd_all[1, :, lanes])
                    halves.append(value.reshape(16, 1, 8, width))
                both = jnp.concatenate(halves, axis=1).reshape(N, N, 16, width)
                sums[part][m, :, :, zz] = both.astype(BF16)
            axis = ORDERS[part][0]
            for k in (1, 2, 3):
                there, target = along(axis, k)
                index = [slice(None)] * 3
                index[axis] = there
                copies[part].append(remote(
                    sums[part].at[m, index[0], index[1], index[2]], in1[part].at[m, k - 1],
                    r_send.at[m, 0, part, k - 1], r_recv.at[m, 0, part, k - 1], target,
                ))
        return copies

    def add(own, incoming):
        return (own.astype(F32) + incoming[0].astype(F32)) + (incoming[1].astype(F32) + incoming[2].astype(F32))

    def reduce_second(m, copies):
        started = [[], [], []]
        for part in range(3):
            received(copies[part])
            axes = ORDERS[part]
            for i in range(N):
                if axes[0] == 0:
                    own = sums[part][m, x, i]
                elif axes[0] == 1:
                    own = sums[part][m, i, y]
                else:
                    own = sums[part][m, i, :, z]
                t1[part][m, i] = add(own, [in1[part][m, q, i] for q in range(3)]).astype(BF16)
            first = axes[1] < axes[2]
            for k in (1, 2, 3):
                there, target = along(axes[1], k)
                src = t1[part].at[m, there] if first else t1[part].at[m, :, there]
                started[part].append(remote(
                    src, in2[part].at[m, k - 1],
                    r_send.at[m, 1, part, k - 1], r_recv.at[m, 1, part, k - 1], target,
                ))
        return started

    def reduce_third(m, copies):
        started = [[], [], []]
        for part in range(3):
            received(copies[part])
            axes = ORDERS[part]
            coord = here[axes[1]]
            own = t1[part][m, coord] if axes[1] < axes[2] else t1[part][m, :, coord]
            t2[part][m] = add(own, [in2[part][m, q] for q in range(3)]).astype(BF16)
            for k in (1, 2, 3):
                there, target = along(axes[2], k)
                started[part].append(remote(
                    t2[part].at[m, there], in3[part].at[m, k - 1],
                    r_send.at[m, 2, part, k - 1], r_recv.at[m, 2, part, k - 1], target,
                ))
        return started

    def finish(m, copies, res_copy):
        received([res_copy])
        pieces = [stats[m, shard, j, z, 4 + q:5 + q] for j in range(N) for q in range(4)]
        across = res_recv[m].astype(F32)
        across = jnp.concatenate([across[0:8], across[8:16]], axis=1)
        base = (res_own[m] + across) / jnp.concatenate(pieces, axis=1)
        for part in range(3):
            received(copies[part])
            own = t2[part][m, here[ORDERS[part][2]]]
            total = add(own, [in3[part][m, q] for q in range(3)])
            for half in range(2):
                start = half * 1024 + STARTS[part]
                lanes = slice(start, start + COLS[part])
                out_ref[m, :, lanes] = (base[:, lanes] + total[half * 8:half * 8 + 8]).astype(BF16)

    attend(0)
    gain_all[core, 0:2] = gain_ref[...]
    gain_all[core, 2:8] = jnp.zeros((6, 128), F32)
    pl.semaphore_wait(barrier, 10)
    a0 = attended_phase(0, 0)
    wo_copy = remote(wo_ref, wo_all.at[core], sib_send.at[0], sib_recv.at[0], sibling)
    resid_copy = remote(resid_ref, resid_all.at[core], sib_send.at[1], sib_recv.at[1], sibling)
    gain_copy = remote(gain_all.at[core], gain_all.at[core], sib_send.at[2], sib_recv.at[2], sibling)
    attend(1)
    received(a0)
    a0 = attended_phase(0, 1)
    a1 = attended_phase(1, 0)
    untangle(0)
    untangle(1)
    received(a1)
    a1 = attended_phase(1, 1)
    choose(0)
    choose(1)
    untangle(2)
    wo_load.wait()
    wo_copy.wait_recv()
    received(a0)
    b0 = project(0)
    wd_copy = remote(wd_ref, wd_all.at[core], sib_send.at[3], sib_recv.at[3], sibling)
    resid_load.wait()
    resid_copy.wait_recv()
    gain_copy.wait_recv()
    gain_row = jnp.concatenate(
        [gain_all[0, 0:1], gain_all[0, 1:2], gain_all[1, 0:1], gain_all[1, 1:2]], axis=1
    )
    resid0 = residual_rows(0)
    received(a1)
    b1 = project(1)
    resid1 = residual_rows(1)
    received(b0)
    mix(0, resid0, gain_row)
    g0 = gather_phase(0, 0)
    untangle(3)
    received(b1)
    mix(1, resid1, gain_row)
    g1 = gather_phase(1, 0)
    received(g0)
    g0 = gather_phase(0, 1)
    untangle(4)
    received(g1)
    g1 = gather_phase(1, 1)
    untangle(5)
    received(g0)
    g0 = gather_phase(0, 2)
    received(g1)
    g1 = gather_phase(1, 2)
    untangle(6)
    untangle(7)
    received(weight_copies.values())
    received(g0)
    h0 = feed(0)
    c0 = residual(0)
    wd_load.wait()
    wd_copy.wait_recv()
    received([h0])
    r0 = down(0)
    received(g1)
    h1 = feed(1)
    c1 = residual(1)
    r0 = reduce_second(0, r0)
    received([h1])
    r1 = down(1)
    r0 = reduce_third(0, r0)
    r1 = reduce_second(1, r1)
    finish(0, r0, c0)
    r1 = reduce_third(1, r1)
    finish(1, r1, c1)

    for copy in all_sends:
        copy.wait_send()


def shards(query, cache, cache_len, row_slot, resid, w_out, norm_gain, w_gate_up, w_down):
    raw = w_gate_up.reshape(8192, 2, 2, 128).transpose(0, 2, 1, 3).reshape(32768, 128)
    vmem = pl.BlockSpec(memory_space=pltpu.VMEM)
    smem = pl.BlockSpec(memory_space=pltpu.SMEM)
    hbm = pl.BlockSpec(memory_space=pl.ANY)
    sem = pltpu.SemaphoreType.DMA
    scratch = [
        pltpu.VMEM((MICRO, 2, 8, 1024, 128), BF16),
        pltpu.VMEM((MICRO, N, N, 16, 1024), BF16),
        pltpu.VMEM((2, 2048, 256), BF16),
        pltpu.VMEM((2, 512, 256), BF16),
        pltpu.VMEM((2, 8, 128), F32),
        pltpu.VMEM((W_SLOTS, 32768 // W_CHUNKS, 128), BF16),
        pltpu.VMEM((2, 8192, 512), BF16),
        pltpu.VMEM((2, 256, 8192), BF16),
        pltpu.VMEM((MICRO, N, 32, 512), BF16),
        pltpu.VMEM((MICRO, 3, 32, 512), BF16),
        pltpu.VMEM((MICRO, N, N, N, 32, 512), BF16),
        pltpu.VMEM((MICRO, N, N, N, 8, 128), F32),
        pltpu.VMEM((128, 1024), F32),
        pltpu.VMEM((MICRO, 2, 128, 512), BF16),
        pltpu.VMEM((MICRO, 3, 128, 128), F32),
    ]
    scratch += [pltpu.VMEM((MICRO, N, N, N, 16, c), BF16) for c in COLS]
    scratch += [pltpu.VMEM((MICRO, 3, N, N, 16, c), BF16) for c in COLS]
    scratch += [pltpu.VMEM((MICRO, N, N, 16, c), BF16) for c in COLS]
    scratch += [pltpu.VMEM((MICRO, 3, N, 16, c), BF16) for c in COLS]
    scratch += [pltpu.VMEM((MICRO, N, 16, c), BF16) for c in COLS]
    scratch += [pltpu.VMEM((MICRO, 3, 16, c), BF16) for c in COLS]
    scratch += [
        pltpu.VMEM((MICRO, 8, 2048), F32),
        pltpu.VMEM((MICRO, 16, 1024), BF16),
        pltpu.VMEM((MICRO, 16, 1024), BF16),
    ]
    scratch += [
        sem((8 + W_CHUNKS,)),
        sem((16,)), sem((16,)),
        sem((MICRO, 2, 2, 3)), sem((MICRO, 2, 2, 3)),
        sem((MICRO, 3)), sem((MICRO, 3)),
        sem((MICRO, 3, 3, 3)), sem((MICRO, 3, 3, 3)),
        sem((MICRO, 3, 3)), sem((MICRO, 3, 3)),
        sem((MICRO, 3, 3, 3)), sem((MICRO, 3, 3, 3)),
    ]
    return pl.pallas_call(
        layer_kernel,
        out_shape=jax.ShapeDtypeStruct((MICRO, 8, 2048), BF16),
        in_specs=[smem, vmem, hbm, vmem, hbm, hbm, vmem, hbm, hbm],
        out_specs=vmem,
        scratch_shapes=scratch,
        compiler_params=pltpu.CompilerParams(
            collective_id=0, has_side_effects=True, vmem_limit_bytes=62 * 1024 * 1024
        ),
        name="layer",
    )(
        cache_len, query, cache.reshape(MICRO, 8, 2, 1024, 128), row_slot, resid.reshape(512, 256), w_out,
        norm_gain.reshape(2, 128), raw, w_down,
    )


def solution(mesh):
    placed = (
        P(None, "grp", ("side", "tp")),
        P(None, "grp", None, ("side", "tp"), None, None),
        P(None, "grp"),
        P(),
        P(None, None, "grp"),
        P(("side", "tp"), "grp"),
        P("grp"),
        P(None, None, ("side", "grp", "tp")),
        P(("side", "grp", "tp"), None),
    )
    return jax.shard_map(
        shards,
        mesh=mesh,
        in_specs=placed,
        out_specs=P(None, "grp", ("side", "tp")),
        check_vma=False,
    )
```

```python
import math

import jax
import jax.numpy as jnp
from jax import lax
from jax.experimental import pallas as pl
from jax.experimental.pallas import tpu as pltpu
from jax.sharding import PartitionSpec as P

MESH = pl.DeviceIdType.MESH
F32 = jnp.float32
BF16 = jnp.bfloat16
EPS = 1e-05
N = 4
MICRO = 2
COLS = (384, 384, 256)
STARTS = (0, 384, 768)
GATHER_PARTS = ((0, 16, 0, 384), (16, 16, 0, 384), (0, 32, 384, 128))
ORDERS = ((0, 1, 2), (1, 2, 0), (2, 0, 1))
W_CHUNKS = 8
W_SLOTS = 3


def dot(a, b):
    return jnp.dot(a, b, preferred_element_type=F32)


def layer_kernel(
    len_ref, query_ref, cache_ref, rows_ref, resid_ref, wo_ref, gain_ref, wg_ref, wd_ref,
    out_ref,
    kv, att_all, wo_all, resid_all, gain_all, w_raw, w_all, wd_all,
    proj_send, proj_recv, gathered, stats, hid, pick,
    sums0, sums1, sums2, via0, via1, via2, in10, in11, in12, t10, t11, t12,
    in20, in21, in22, t20, t21, t22, in30, in31, in32,
    res_own, res_send, res_recv,
    local_sem, sib_send, sib_recv, a_send, a_recv, b_send, b_recv,
    g_send, g_recv, s_send, s_recv, r_send, r_recv,
):
    g = lax.axis_index("grp")
    side = lax.axis_index("side")
    tp = lax.axis_index("tp")
    core = lax.rem(g, 2)
    y = lax.rem(g // 2, N)
    x = g // 8
    z = tp * 2 + side
    here = (x, y, z)
    xy = x * N + y
    shard = side * 2 + tp

    def device(cx, cy, cz, cc):
        return {"side": lax.rem(cz, 2), "grp": (cx * N + cy) * 2 + cc, "tp": cz // 2}

    def along(axis, k):
        moved = list(here)
        moved[axis] = lax.rem(here[axis] + k, N)
        return moved[axis], device(moved[0], moved[1], moved[2], core)

    sibling = device(x, y, z, 1 - core)
    all_sends = []

    def remote(src, dst, send, recv, target):
        copy = pltpu.make_async_remote_copy(
            src_ref=src, dst_ref=dst, send_sem=send, recv_sem=recv,
            device_id=target, device_id_type=MESH,
        )
        copy.start()
        all_sends.append(copy)
        return copy

    def local(src, dst, sem):
        copy = pltpu.make_async_copy(src, dst, sem)
        copy.start()
        return copy

    def received(copies):
        for copy in copies:
            copy.wait_recv()

    barrier = pltpu.get_barrier_semaphore()
    for axis in range(3):
        for k in (1, 2, 3):
            pl.semaphore_signal(barrier, inc=1, device_id=along(axis, k)[1], device_id_type=MESH)
    pl.semaphore_signal(barrier, inc=1, device_id=sibling, device_id_type=MESH)

    def load_kv(m):
        return [local(cache_ref.at[m, :, i], kv.at[m, i], local_sem.at[m * 2 + i]) for i in range(2)]

    kv_loads = {0: load_kv(0), 1: load_kv(1)}
    raw_rows = w_raw.shape[1]

    def load_raw(chunk):
        return local(
            wg_ref.at[pl.ds(chunk * raw_rows, raw_rows)], w_raw.at[chunk % W_SLOTS], local_sem.at[8 + chunk]
        )

    raw_loads = {}
    other_loads = {}

    def load_rest():
        other_loads["wo"] = local(wo_ref, wo_all.at[core], local_sem.at[4])
        other_loads["resid"] = local(resid_ref, resid_all.at[core], local_sem.at[5])
        for chunk in range(W_SLOTS):
            raw_loads[chunk] = load_raw(chunk)

    def attend(m):
        queries = query_ref[m].astype(F32)
        heads = queries.shape[1] // 128
        stacked = jnp.concatenate([queries[:, h * 128:(h + 1) * 128] for h in range(heads)], axis=0).astype(BF16)
        slot_id = lax.broadcasted_iota(jnp.int32, (heads * 8, 1), 0) % 8
        live = jnp.zeros((heads * 8, 1), jnp.int32)
        for s in range(8):
            live = jnp.where(slot_id == s, len_ref[m, s], live)
        kv_loads[m][0].wait()
        if m == 0:
            load_rest()
        scores = None
        for s in range(8):
            one = lax.dot_general(stacked, kv[m, 0, s], (((1,), (1,)), ((), ())), preferred_element_type=F32)
            scores = one if s == 0 else jnp.where(slot_id == s, one, scores)
        position = lax.broadcasted_iota(jnp.int32, scores.shape, 1)
        scores = jnp.where(position < live, scores * (1.0 / math.sqrt(128)), -jnp.inf)
        top = jnp.max(scores, axis=1, keepdims=True)
        raised = jnp.exp(scores - top)
        total = jnp.sum(raised, axis=1, keepdims=True)
        weights = (raised / total).astype(BF16)
        kv_loads[m][1].wait()
        mixed = None
        for s in range(8):
            one = dot(weights, kv[m, 1, s])
            mixed = one if s == 0 else jnp.where(slot_id == s, one, mixed)
        halves = []
        for half in range(2):
            tiles = [mixed[(half * 8 + h) * 8:(half * 8 + h) * 8 + 8] for h in range(8)]
            halves.append(jnp.concatenate(tiles, axis=1))
        att_all[m, x, y] = jnp.concatenate(halves, axis=0).astype(BF16)

    def attended_phase(m, phase):
        copies = []
        for part in range(2):
            cols = pl.ds(part * 512, 512)
            axis = part if phase == 0 else 1 - part
            index = [x, y]
            if phase == 1:
                index[part] = slice(None)
            ref = att_all.at[m, index[0], index[1], :, cols]
            for k in (1, 2, 3):
                copies.append(remote(
                    ref, ref, a_send.at[m, phase, part, k - 1], a_recv.at[m, phase, part, k - 1], along(axis, k)[1]
                ))
        return copies

    p_out = lax.broadcasted_iota(jnp.int32, (256, 256), 0)
    p_in = lax.broadcasted_iota(jnp.int32, (256, 256), 1)
    order = jnp.where(p_in == (p_out % 64) * 4 + p_out // 64, 1.0, 0.0).astype(BF16)
    weight_copies = {}

    def untangle(chunk):
        raw_loads[chunk].wait()
        span = raw_rows // 512
        slot = chunk % W_SLOTS

        tiles = raw_rows // 256
        mixed = jnp.concatenate([w_raw[slot, q * 256:(q + 1) * 256] for q in range(tiles)], axis=1)
        apart = dot(order, mixed)
        for l in range(2):
            for c in range(2):
                rows = slice((l * 2 + c) * 64, (l * 2 + c) * 64 + 64)
                lanes = pl.ds(c * 256 + l * 128, 128)
                for q in range(tiles):
                    base = (chunk * tiles + q) * 64
                    w_all[core, pl.ds(base, 64), lanes] = apart[rows, q * 128:(q + 1) * 128].astype(BF16)
        if chunk + W_SLOTS < W_CHUNKS:
            raw_loads[chunk + W_SLOTS] = load_raw(chunk + W_SLOTS)
        block = w_all.at[core, pl.ds(chunk * span * 128, span * 128)]
        weight_copies[chunk] = remote(block, block, sib_send.at[4 + chunk], sib_recv.at[4 + chunk], sibling)

    def slot_of(r, parity):
        return ((r // 8) * 2 + parity) * 8 + r % 8

    def choose(m):
        r = lax.broadcasted_iota(jnp.int32, (128, 256), 0)
        for i, parity in enumerate((core, 1 - core)):
            hit = jnp.where(slot_of(r, parity) == rows_ref[m:m + 1, :], 1.0, 0.0)
            turned = jnp.concatenate([jnp.transpose(hit[:, 0:128]), jnp.transpose(hit[:, 128:256])], axis=0)
            turned = turned.reshape(16, 2, 8, 128)
            even, odd = turned[:, 0].reshape(128, 128), turned[:, 1].reshape(128, 128)
            pick[m, i] = jnp.where(core == 0, even, odd)
            if i == 0:
                pick[m, 2] = jnp.where(core == 0, odd, even)

    def project(m):
        blocks = att_all[m].astype(F32).reshape(16, 2, 8, 1024)
        rows = jnp.concatenate([blocks[:, 0].reshape(128, 1024), blocks[:, 1].reshape(128, 1024)], axis=1).astype(BF16)
        for c in range(2):
            proj_send[m, :, :, c * 256:(c + 1) * 256] = dot(rows, wo_all[c]).astype(BF16).reshape(N, 32, 256)
        copies = []
        for k in (1, 2, 3):
            there, target = along(2, k)
            copies.append(remote(
                proj_send.at[m, there], proj_recv.at[m, k - 1], b_send.at[m, k - 1], b_recv.at[m, k - 1], target
            ))
        return copies

    def residual_rows(m):
        r = z * 32 + lax.broadcasted_iota(jnp.int32, (32, 256), 0)
        served = jnp.where(slot_of(r, core) == rows_ref[m:m + 1, :], 1.0, 0.0).astype(BF16)
        return jnp.concatenate([dot(served, resid_all[c, m * 256:(m + 1) * 256]) for c in range(2)], axis=1)

    def mix(m, resid_rows, gain_row):
        mixed = resid_rows + (
            (proj_send[m, z].astype(F32) + proj_recv[m, 0].astype(F32))
            + (proj_recv[m, 1].astype(F32) + proj_recv[m, 2].astype(F32))
        )
        gathered[m, x, y, z] = (mixed * gain_row).astype(BF16)
        squares = jnp.sum(mixed * mixed, axis=1, keepdims=True)
        tall = jnp.concatenate([jnp.broadcast_to(squares, (32, 128)), jnp.zeros((96, 128), F32)], axis=0)
        stats[m, x, y, z, 0:4] = jnp.transpose(tall)[0:4]
        stats[m, x, y, z, 4:6] = gain_all[0, 0:2]
        stats[m, x, y, z, 6:8] = gain_all[1, 0:2]

    def gather_phase(m, phase):
        copies = []
        for part, (row, rows, col, cols) in enumerate(GATHER_PARTS):
            axes = ORDERS[part]
            index = list(here)
            for done in axes[:phase]:
                index[done] = slice(None)
            block = gathered.at[m, index[0], index[1], index[2], pl.ds(row, rows), pl.ds(col, cols)]
            for k in (1, 2, 3):
                target = along(axes[phase], k)[1]
                copies.append(remote(
                    block, block, g_send.at[m, phase, part, k - 1], g_recv.at[m, phase, part, k - 1], target
                ))
                if part == 2:
                    tile = stats.at[m, index[0], index[1], index[2]]
                    copies.append(remote(
                        tile, tile, s_send.at[m, phase, k - 1], s_recv.at[m, phase, k - 1], target
                    ))
        return copies

    def gather_block(m, part, coord, half):
        axis = ORDERS[part][2]
        row, rows, col, cols = GATHER_PARTS[part]
        index = [slice(None)] * 3
        index[min(ORDERS[part][:2])] = pl.ds(half * 2, 2)
        index[axis] = coord
        return gathered.at[m, index[0], index[1], index[2], pl.ds(row, rows), pl.ds(col, cols)]

    def gather_step(m, part, coord, half, k, slot):
        block = gather_block(m, part, coord, half)
        return remote(
            block, block, g_send.at[m, 2, part, slot], g_recv.at[m, 2, part, slot], along(ORDERS[part][2], k)[1]
        )

    def gather_last(m):
        own = [here[ORDERS[part][2]] for part in range(3)]
        early = [
            (gather_step(m, part, own[part], 0, 1, 0), gather_step(m, part, own[part], 1, 3, 1)) for part in range(3)
        ]
        late = []
        for part in range(3):
            late.append(gather_step(m, part, own[part], 1, 1, 2))
            late.append(gather_step(m, part, own[part], 0, 3, 3))
        for k in (1, 2, 3):
            tile = stats.at[m, :, y]
            late.append(remote(tile, tile, s_send.at[m, 2, k - 1], s_recv.at[m, 2, k - 1], along(1, k)[1]))
        return early, late

    def gather_pass(m, early, late):
        for part in range(3):
            axis = ORDERS[part][2]
            early[part][0].wait_recv()
            late.append(gather_step(m, part, along(axis, 3)[0], 0, 1, 4))
            early[part][1].wait_recv()
            late.append(gather_step(m, part, along(axis, 1)[0], 1, 3, 5))

    def feed(m):
        total = jnp.sum(stats[m].reshape(16, N, 8, 128), axis=0)
        columns = []
        for zz in range(N):
            spread = jnp.transpose(jnp.broadcast_to(total[zz, 0:1], (128, 128)))
            columns.append(spread[0:32])
        row_scale = lax.rsqrt(jnp.concatenate(columns, axis=0) * (1.0 / 8192) + EPS)
        row_scale = jnp.concatenate([row_scale, row_scale], axis=1)
        features = jnp.concatenate(
            [gathered[m, i, j].reshape(128, 512) for i in range(N) for j in range(N)], axis=1
        )
        for p in range(2):
            gate = dot(features, w_all[p, :, 0:256]) * row_scale
            up = dot(features, w_all[p, :, 256:512]) * row_scale
            hid[m, core, :, p * 256:(p + 1) * 256] = (gate / (1.0 + jnp.exp(-gate)) * up).astype(BF16)
        block = hid.at[m, core]
        return remote(block, block, sib_send.at[12 + m], sib_recv.at[12 + m], sibling)

    def residual(m):
        row = pl.multiple_of(xy * 8, 8)
        wanted = jnp.concatenate([pick[m, 0, pl.ds(row, 8), :], pick[m, 2, pl.ds(row, 8), :]], axis=0).astype(BF16)
        found = [dot(wanted, gathered[m, shard, j].reshape(128, 512)) for j in range(N)]
        found = jnp.concatenate(found, axis=1)
        res_own[m] = found[0:8]
        res_send[m] = jnp.concatenate([found[8:16, 0:1024], found[8:16, 1024:2048]], axis=0).astype(BF16)
        return remote(res_send.at[m], res_recv.at[m], sib_send.at[14 + m], sib_recv.at[14 + m], sibling)

    sums = (sums0, sums1, sums2)
    via = (via0, via1, via2)
    in1 = (in10, in11, in12)
    t1 = (t10, t11, t12)
    in2 = (in20, in21, in22)
    t2 = (t20, t21, t22)
    in3 = (in30, in31, in32)

    def sum_index(part, coord, half):
        axis = ORDERS[part][0]
        index = [slice(None)] * 3
        index[1 if axis == 0 else 0] = pl.ds(half * 2, 2)
        index[axis] = coord
        return index

    def reduce_step(m, part, coord, half, dst, k, slot):
        index = sum_index(part, coord, half)
        return remote(
            sums[part].at[m, index[0], index[1], index[2]], dst,
            r_send.at[m, 0, part, slot], r_recv.at[m, 0, part, slot], along(ORDERS[part][0], k)[1],
        )

    def down(m):
        other = jnp.where(core == 0, hid[m, 1].astype(F32), hid[m, 0].astype(F32)).astype(BF16)
        ours = dot(pick[m, 0].astype(BF16), hid[m, core]) + dot(pick[m, 1].astype(BF16), other)
        ours = ours.astype(BF16)
        copies = [[], [], []]
        for part in range(3):
            width = COLS[part]
            for zz in range(N):
                base = ((zz % 2) * 2 + zz // 2) * 2048 + STARTS[part]
                halves = []
                for half in range(2):
                    lanes = pl.ds(base + half * 1024, width)
                    value = dot(ours[:, 0:256], wd_all[0, :, lanes]) + dot(ours[:, 256:512], wd_all[1, :, lanes])
                    halves.append(value.reshape(16, 1, 8, width))
                both = jnp.concatenate(halves, axis=1).reshape(N, N, 16, width)
                sums[part][m, :, :, zz] = both.astype(BF16)
            far = along(ORDERS[part][0], 2)[0]
            ahead, back = along(ORDERS[part][0], 1)[0], along(ORDERS[part][0], 3)[0]
            copies[part] = [
                reduce_step(m, part, far, 0, via[part].at[m, 0], 1, 0),
                reduce_step(m, part, far, 1, via[part].at[m, 1], 3, 1),
                reduce_step(m, part, ahead, 1, in1[part].at[m, 0, pl.ds(2, 2)], 1, 2),
                reduce_step(m, part, back, 0, in1[part].at[m, 1, pl.ds(0, 2)], 3, 3),
            ]
        return copies

    def reduce_pass(m, copies):
        for part in range(3):
            for half, k in ((0, 1), (1, 3)):
                there = along(ORDERS[part][0], k)[0]
                copies[part][half].wait_recv()
                index = sum_index(part, there, half)
                own = sums[part][m, index[0], index[1], index[2]].astype(F32)
                sums[part][m, index[0], index[1], index[2]] = (own + via[part][m, half].astype(F32)).astype(BF16)
                copies[part].append(reduce_step(
                    m, part, there, half, in1[part].at[m, half, pl.ds(half * 2, 2)], k, 4 + half
                ))

    def add(own, incoming):
        total = own.astype(F32)
        for term in incoming:
            total = total + term.astype(F32)
        return total

    def reduce_second(m, copies):
        started = [[], [], []]
        for part in range(3):
            received(copies[part][2:])
            axes = ORDERS[part]
            for i in range(N):
                if axes[0] == 0:
                    own = sums[part][m, x, i]
                elif axes[0] == 1:
                    own = sums[part][m, i, y]
                else:
                    own = sums[part][m, i, :, z]
                t1[part][m, i] = add(own, [in1[part][m, q, i] for q in range(2)]).astype(BF16)
            first = axes[1] < axes[2]
            for k in (1, 2, 3):
                there, target = along(axes[1], k)
                src = t1[part].at[m, there] if first else t1[part].at[m, :, there]
                started[part].append(remote(
                    src, in2[part].at[m, k - 1],
                    r_send.at[m, 1, part, k - 1], r_recv.at[m, 1, part, k - 1], target,
                ))
        return started

    def reduce_third(m, copies):
        started = [[], [], []]
        for part in range(3):
            received(copies[part])
            axes = ORDERS[part]
            coord = here[axes[1]]
            own = t1[part][m, coord] if axes[1] < axes[2] else t1[part][m, :, coord]
            t2[part][m] = add(own, [in2[part][m, q] for q in range(3)]).astype(BF16)
            for k in (1, 2, 3):
                there, target = along(axes[2], k)
                started[part].append(remote(
                    t2[part].at[m, there], in3[part].at[m, k - 1],
                    r_send.at[m, 2, part, k - 1], r_recv.at[m, 2, part, k - 1], target,
                ))
        return started

    def finish(m, copies, res_copy):
        received([res_copy])
        pieces = [stats[m, shard, j, z, 4 + q:5 + q] for j in range(N) for q in range(4)]
        across = res_recv[m].astype(F32)
        across = jnp.concatenate([across[0:8], across[8:16]], axis=1)
        base = (res_own[m] + across) / jnp.concatenate(pieces, axis=1)
        for part in range(3):
            received(copies[part])
            own = t2[part][m, here[ORDERS[part][2]]]
            total = add(own, [in3[part][m, q] for q in range(3)])
            for half in range(2):
                start = half * 1024 + STARTS[part]
                lanes = slice(start, start + COLS[part])
                out_ref[m, :, lanes] = (base[:, lanes] + total[half * 8:half * 8 + 8]).astype(BF16)

    attend(0)
    gain_all[core, 0:2] = gain_ref[...]
    gain_all[core, 2:8] = jnp.zeros((6, 128), F32)
    pl.semaphore_wait(barrier, 10)
    a0 = attended_phase(0, 0)
    wo_copy = remote(wo_ref, wo_all.at[core], sib_send.at[0], sib_recv.at[0], sibling)
    resid_copy = remote(resid_ref, resid_all.at[core], sib_send.at[1], sib_recv.at[1], sibling)
    gain_copy = remote(gain_all.at[core], gain_all.at[core], sib_send.at[2], sib_recv.at[2], sibling)
    attend(1)
    a1 = attended_phase(1, 0)
    received(a0)
    a0 = attended_phase(0, 1)
    wd_load = local(wd_ref, wd_all.at[core], local_sem.at[6])
    wd_copy = remote(wd_ref, wd_all.at[core], sib_send.at[3], sib_recv.at[3], sibling)
    untangle(0)
    untangle(1)
    untangle(2)
    received(a1)
    a1 = attended_phase(1, 1)
    choose(0)
    choose(1)
    untangle(3)
    other_loads["wo"].wait()
    wo_copy.wait_recv()
    received(a0)
    b0 = project(0)
    other_loads["resid"].wait()
    resid_copy.wait_recv()
    gain_copy.wait_recv()
    gain_row = jnp.concatenate(
        [gain_all[0, 0:1], gain_all[0, 1:2], gain_all[1, 0:1], gain_all[1, 1:2]], axis=1
    )
    resid0 = residual_rows(0)
    untangle(4)
    received(a1)
    b1 = project(1)
    resid1 = residual_rows(1)
    untangle(5)
    received(b0)
    mix(0, resid0, gain_row)
    g0 = gather_phase(0, 0)
    received(b1)
    mix(1, resid1, gain_row)
    g1 = gather_phase(1, 0)
    untangle(6)
    received(g0)
    g0 = gather_phase(0, 1)
    received(g1)
    g1 = gather_phase(1, 1)
    untangle(7)
    received(g0)
    g0, l0 = gather_last(0)
    received(g1)
    gather_pass(0, g0, l0)
    g1, l1 = gather_last(1)
    gather_pass(1, g1, l1)
    received(weight_copies.values())
    received(l0)
    h0 = feed(0)
    c0 = residual(0)
    wd_load.wait()
    wd_copy.wait_recv()
    received([h0])
    r0 = down(0)
    received(l1)
    h1 = feed(1)
    c1 = residual(1)
    reduce_pass(0, r0)
    received([h1])
    r1 = down(1)
    r0 = reduce_second(0, r0)
    reduce_pass(1, r1)
    r0 = reduce_third(0, r0)
    r1 = reduce_second(1, r1)
    finish(0, r0, c0)
    r1 = reduce_third(1, r1)
    finish(1, r1, c1)

    for copy in all_sends:
        copy.wait_send()


def shards(query, cache, cache_len, row_slot, resid, w_out, norm_gain, w_gate_up, w_down):
    raw = w_gate_up.reshape(8192, 2, 2, 128).transpose(0, 2, 1, 3).reshape(32768, 128)
    vmem = pl.BlockSpec(memory_space=pltpu.VMEM)
    smem = pl.BlockSpec(memory_space=pltpu.SMEM)
    hbm = pl.BlockSpec(memory_space=pl.ANY)
    sem = pltpu.SemaphoreType.DMA
    scratch = [
        pltpu.VMEM((MICRO, 2, 8, 1024, 128), BF16),
        pltpu.VMEM((MICRO, N, N, 16, 1024), BF16),
        pltpu.VMEM((2, 2048, 256), BF16),
        pltpu.VMEM((2, 512, 256), BF16),
        pltpu.VMEM((2, 8, 128), F32),
        pltpu.VMEM((W_SLOTS, 32768 // W_CHUNKS, 128), BF16),
        pltpu.VMEM((2, 8192, 512), BF16),
        pltpu.VMEM((2, 256, 8192), BF16),
        pltpu.VMEM((MICRO, N, 32, 512), BF16),
        pltpu.VMEM((MICRO, 3, 32, 512), BF16),
        pltpu.VMEM((MICRO, N, N, N, 32, 512), BF16),
        pltpu.VMEM((MICRO, N, N, N, 8, 128), F32),
        pltpu.VMEM((MICRO, 2, 128, 512), BF16),
        pltpu.VMEM((MICRO, 3, 128, 128), F32),
    ]
    scratch += [pltpu.VMEM((MICRO, N, N, N, 16, c), BF16) for c in COLS]
    scratch += [pltpu.VMEM((MICRO, 2, 2, N, 16, c), BF16) for c in COLS]
    scratch += [pltpu.VMEM((MICRO, 2, N, N, 16, c), BF16) for c in COLS]
    scratch += [pltpu.VMEM((MICRO, N, N, 16, c), BF16) for c in COLS]
    scratch += [pltpu.VMEM((MICRO, 3, N, 16, c), BF16) for c in COLS]
    scratch += [pltpu.VMEM((MICRO, N, 16, c), BF16) for c in COLS]
    scratch += [pltpu.VMEM((MICRO, 3, 16, c), BF16) for c in COLS]
    scratch += [
        pltpu.VMEM((MICRO, 8, 2048), F32),
        pltpu.VMEM((MICRO, 16, 1024), BF16),
        pltpu.VMEM((MICRO, 16, 1024), BF16),
    ]
    scratch += [
        sem((8 + W_CHUNKS,)),
        sem((16,)), sem((16,)),
        sem((MICRO, 2, 2, 3)), sem((MICRO, 2, 2, 3)),
        sem((MICRO, 3)), sem((MICRO, 3)),
        sem((MICRO, 3, 3, 6)), sem((MICRO, 3, 3, 6)),
        sem((MICRO, 3, 3)), sem((MICRO, 3, 3)),
        sem((MICRO, 3, 3, 6)), sem((MICRO, 3, 3, 6)),
    ]
    return pl.pallas_call(
        layer_kernel,
        out_shape=jax.ShapeDtypeStruct((MICRO, 8, 2048), BF16),
        in_specs=[smem, vmem, hbm, vmem, hbm, hbm, vmem, hbm, hbm],
        out_specs=vmem,
        scratch_shapes=scratch,
        compiler_params=pltpu.CompilerParams(
            collective_id=0, has_side_effects=True, vmem_limit_bytes=62 * 1024 * 1024
        ),
        name="layer",
    )(
        cache_len, query, cache.reshape(MICRO, 8, 2, 1024, 128), row_slot, resid.reshape(512, 256), w_out,
        norm_gain.reshape(2, 128), raw, w_down,
    )


def solution(mesh):
    placed = (
        P(None, "grp", ("side", "tp")),
        P(None, "grp", None, ("side", "tp"), None, None),
        P(None, "grp"),
        P(),
        P(None, None, "grp"),
        P(("side", "tp"), "grp"),
        P("grp"),
        P(None, None, ("side", "grp", "tp")),
        P(("side", "grp", "tp"), None),
    )
    return jax.shard_map(
        shards,
        mesh=mesh,
        in_specs=placed,
        out_specs=P(None, "grp", ("side", "tp")),
        check_vma=False,
    )
```

```python
import math

import jax
import jax.numpy as jnp
from jax import lax
from jax.experimental import pallas as pl
from jax.experimental.pallas import tpu as pltpu
from jax.sharding import PartitionSpec as P

MESH = pl.DeviceIdType.MESH
F32 = jnp.float32
BF16 = jnp.bfloat16
EPS = 1e-05
N = 4
MICRO = 2
COLS = (384, 384, 256)
STARTS = (0, 384, 768)
GATHER_PARTS = ((0, 16, 0, 384), (16, 16, 0, 384), (0, 32, 384, 128))
ORDERS = ((0, 1, 2), (1, 2, 0), (2, 0, 1))
W_CHUNKS = 8
W_SLOTS = 3


def dot(a, b):
    return jnp.dot(a, b, preferred_element_type=F32)


def layer_kernel(
    len_ref, query_in, cache_ref, rows_in, resid_ref, wo_ref, gain_in, wg_ref, wd_ref,
    out_ref,
    query_ref, rows_ref, gain_ref, kv, att_all, wo_all, resid_all, gain_all, w_raw, w_all, wd_all,
    proj_send, proj_recv, gathered, stats, hid, pick,
    sums0, sums1, sums2, via0, via1, via2, in10, in11, in12, t10, t11, t12,
    in20, in21, in22, t20, t21, t22, in30, in31, in32,
    res_own, res_send, res_recv,
    local_sem, sib_send, sib_recv, a_send, a_recv, b_send, b_recv,
    g_send, g_recv, s_send, s_recv, r_send, r_recv,
):
    g = lax.axis_index("grp")
    side = lax.axis_index("side")
    tp = lax.axis_index("tp")
    core = lax.rem(g, 2)
    y = lax.rem(g // 2, N)
    x = g // 8
    z = tp * 2 + side
    here = (x, y, z)
    xy = x * N + y
    shard = side * 2 + tp

    def device(cx, cy, cz, cc):
        return {"side": lax.rem(cz, 2), "grp": (cx * N + cy) * 2 + cc, "tp": cz // 2}

    def along(axis, k):
        moved = list(here)
        moved[axis] = lax.rem(here[axis] + k, N)
        return moved[axis], device(moved[0], moved[1], moved[2], core)

    sibling = device(x, y, z, 1 - core)
    all_sends = []

    def remote(src, dst, send, recv, target):
        copy = pltpu.make_async_remote_copy(
            src_ref=src, dst_ref=dst, send_sem=send, recv_sem=recv,
            device_id=target, device_id_type=MESH,
        )
        copy.start()
        all_sends.append(copy)
        return copy

    def local(src, dst, sem):
        copy = pltpu.make_async_copy(src, dst, sem)
        copy.start()
        return copy

    def drain(count):
        for copy in all_sends[:count]:
            copy.wait_send()
        del all_sends[:count]

    def received(copies):
        for copy in copies:
            copy.wait_recv()

    query_load = local(query_in, query_ref, local_sem.at[8 + W_CHUNKS])

    barrier = pltpu.get_barrier_semaphore()
    for axis in range(3):
        for k in (1, 2, 3):
            pl.semaphore_signal(barrier, inc=1, device_id=along(axis, k)[1], device_id_type=MESH)
    pl.semaphore_signal(barrier, inc=1, device_id=sibling, device_id_type=MESH)

    def load_kv(m):
        return [local(cache_ref.at[m, :, i], kv.at[m, i], local_sem.at[m * 2 + i]) for i in range(2)]

    kv_loads = {0: load_kv(0), 1: load_kv(1)}
    rows_load = local(rows_in, rows_ref, local_sem.at[7])
    gain_load = local(gain_in, gain_ref, local_sem.at[9 + W_CHUNKS])
    raw_rows = w_raw.shape[1]

    def load_raw(chunk):
        return local(
            wg_ref.at[pl.ds(chunk * raw_rows, raw_rows)], w_raw.at[chunk % W_SLOTS], local_sem.at[8 + chunk]
        )

    raw_loads = {}
    other_loads = {}

    def load_rest():
        other_loads["wo"] = local(wo_ref, wo_all.at[core], local_sem.at[4])
        other_loads["resid"] = local(resid_ref, resid_all.at[core], local_sem.at[5])
        for chunk in range(W_SLOTS):
            raw_loads[chunk] = load_raw(chunk)

    def attend(m):
        if m == 0:
            query_load.wait()
        queries = query_ref[m].astype(F32)
        heads = queries.shape[1] // 128
        stacked = jnp.concatenate([queries[:, h * 128:(h + 1) * 128] for h in range(heads)], axis=0).astype(BF16)
        slot_id = lax.broadcasted_iota(jnp.int32, (heads * 8, 1), 0) % 8
        live = jnp.zeros((heads * 8, 1), jnp.int32)
        for s in range(8):
            live = jnp.where(slot_id == s, len_ref[m, s], live)
        kv_loads[m][0].wait()
        if m == 0:
            load_rest()
        scores = None
        for s in range(8):
            one = lax.dot_general(stacked, kv[m, 0, s], (((1,), (1,)), ((), ())), preferred_element_type=F32)
            scores = one if s == 0 else jnp.where(slot_id == s, one, scores)
        position = lax.broadcasted_iota(jnp.int32, scores.shape, 1)
        scores = jnp.where(position < live, scores * (1.0 / math.sqrt(128)), -jnp.inf)
        top = jnp.max(scores, axis=1, keepdims=True)
        raised = jnp.exp(scores - top)
        total = jnp.sum(raised, axis=1, keepdims=True)
        weights = (raised / total).astype(BF16)
        kv_loads[m][1].wait()
        mixed = None
        for s in range(8):
            one = dot(weights, kv[m, 1, s])
            mixed = one if s == 0 else jnp.where(slot_id == s, one, mixed)
        halves = []
        for half in range(2):
            tiles = [mixed[(half * 8 + h) * 8:(half * 8 + h) * 8 + 8] for h in range(8)]
            halves.append(jnp.concatenate(tiles, axis=1))
        att_all[m, x, y] = jnp.concatenate(halves, axis=0).astype(BF16)

    def attended_phase(m, phase):
        copies = []
        for part in range(2):
            cols = pl.ds(part * 512, 512)
            axis = part if phase == 0 else 1 - part
            index = [x, y]
            if phase == 1:
                index[part] = slice(None)
            ref = att_all.at[m, index[0], index[1], :, cols]
            for k in (1, 2, 3):
                copies.append(remote(
                    ref, ref, a_send.at[m, phase, part, k - 1], a_recv.at[m, phase, part, k - 1], along(axis, k)[1]
                ))
        return copies

    p_out = lax.broadcasted_iota(jnp.int32, (256, 256), 0)
    p_in = lax.broadcasted_iota(jnp.int32, (256, 256), 1)
    order = jnp.where(p_in == (p_out % 64) * 4 + p_out // 64, 1.0, 0.0).astype(BF16)
    weight_copies = {}

    def untangle(chunk):
        raw_loads[chunk].wait()
        slot = chunk % W_SLOTS

        tiles = raw_rows // 256
        mixed = jnp.concatenate([w_raw[slot, q * 256:(q + 1) * 256] for q in range(tiles)], axis=1)
        apart = dot(order, mixed)
        for l in range(2):
            for c in range(2):
                rows = slice((l * 2 + c) * 64, (l * 2 + c) * 64 + 64)
                lanes = pl.ds(c * 256 + l * 128, 128)
                for q in range(tiles):
                    base = (chunk * tiles + q) * 64
                    w_all[core, pl.ds(base, 64), lanes] = apart[rows, q * 128:(q + 1) * 128].astype(BF16)
        if chunk + W_SLOTS < W_CHUNKS:
            raw_loads[chunk + W_SLOTS] = load_raw(chunk + W_SLOTS)

    def share(chunk):
        span = raw_rows // 512
        block = w_all.at[core, pl.ds(chunk * span * 128, span * 128)]
        weight_copies[chunk] = remote(block, block, sib_send.at[4 + chunk], sib_recv.at[4 + chunk], sibling)

    def slot_of(r, parity):
        return ((r // 8) * 2 + parity) * 8 + r % 8

    def choose(m):
        r = lax.broadcasted_iota(jnp.int32, (128, 256), 0)
        for i, parity in enumerate((core, 1 - core)):
            hit = jnp.where(slot_of(r, parity) == rows_ref[m:m + 1, :], 1.0, 0.0)
            turned = jnp.concatenate([jnp.transpose(hit[:, 0:128]), jnp.transpose(hit[:, 128:256])], axis=0)
            turned = turned.reshape(16, 2, 8, 128)
            even, odd = turned[:, 0].reshape(128, 128), turned[:, 1].reshape(128, 128)
            pick[m, i] = jnp.where(core == 0, even, odd)
            if i == 0:
                pick[m, 2] = jnp.where(core == 0, odd, even)

    def project(m):
        blocks = att_all[m].astype(F32).reshape(16, 2, 8, 1024)
        rows = jnp.concatenate([blocks[:, 0].reshape(128, 1024), blocks[:, 1].reshape(128, 1024)], axis=1).astype(BF16)
        for c in range(2):
            proj_send[m, :, :, c * 256:(c + 1) * 256] = dot(rows, wo_all[c]).astype(BF16).reshape(N, 32, 256)
        copies = []
        for k in (1, 2, 3):
            there, target = along(2, k)
            copies.append(remote(
                proj_send.at[m, there], proj_recv.at[m, k - 1], b_send.at[m, k - 1], b_recv.at[m, k - 1], target
            ))
        return copies

    def residual_rows(m):
        r = z * 32 + lax.broadcasted_iota(jnp.int32, (32, 256), 0)
        served = jnp.where(slot_of(r, core) == rows_ref[m:m + 1, :], 1.0, 0.0).astype(BF16)
        return jnp.concatenate([dot(served, resid_all[c, m * 256:(m + 1) * 256]) for c in range(2)], axis=1)

    def mix(m, resid_rows, gain_row):
        mixed = resid_rows + (
            (proj_send[m, z].astype(F32) + proj_recv[m, 0].astype(F32))
            + (proj_recv[m, 1].astype(F32) + proj_recv[m, 2].astype(F32))
        )
        gathered[m, x, y, z] = (mixed * gain_row).astype(BF16)
        squares = jnp.sum(mixed * mixed, axis=1, keepdims=True)
        tall = jnp.concatenate([jnp.broadcast_to(squares, (32, 128)), jnp.zeros((96, 128), F32)], axis=0)
        stats[m, x, y, z, 0:4] = jnp.transpose(tall)[0:4]
        stats[m, x, y, z, 4:6] = gain_all[0, 0:2]
        stats[m, x, y, z, 6:8] = gain_all[1, 0:2]

    def gather_phase(m, phase):
        copies = []
        for part, (row, rows, col, cols) in enumerate(GATHER_PARTS):
            axes = ORDERS[part]
            index = list(here)
            for done in axes[:phase]:
                index[done] = slice(None)
            block = gathered.at[m, index[0], index[1], index[2], pl.ds(row, rows), pl.ds(col, cols)]
            for k in (1, 2, 3):
                target = along(axes[phase], k)[1]
                copies.append(remote(
                    block, block, g_send.at[m, phase, part, k - 1], g_recv.at[m, phase, part, k - 1], target
                ))
                if part == 2:
                    tile = stats.at[m, index[0], index[1], index[2]]
                    copies.append(remote(
                        tile, tile, s_send.at[m, phase, k - 1], s_recv.at[m, phase, k - 1], target
                    ))
        return copies

    def gather_block(m, part, coord, half):
        axis = ORDERS[part][2]
        row, rows, col, cols = GATHER_PARTS[part]
        index = [slice(None)] * 3
        index[min(ORDERS[part][:2])] = pl.ds(half * 2, 2)
        index[axis] = coord
        return gathered.at[m, index[0], index[1], index[2], pl.ds(row, rows), pl.ds(col, cols)]

    def gather_step(m, part, coord, half, k, slot):
        block = gather_block(m, part, coord, half)
        return remote(
            block, block, g_send.at[m, 2, part, slot], g_recv.at[m, 2, part, slot], along(ORDERS[part][2], k)[1]
        )

    def gather_last(m):
        own = [here[ORDERS[part][2]] for part in range(3)]
        early = [
            (gather_step(m, part, own[part], 0, 1, 0), gather_step(m, part, own[part], 1, 3, 1)) for part in range(3)
        ]
        late = []
        for part in range(3):
            late.append(gather_step(m, part, own[part], 1, 1, 2))
            late.append(gather_step(m, part, own[part], 0, 3, 3))
        for k in (1, 2, 3):
            tile = stats.at[m, :, y]
            late.append(remote(tile, tile, s_send.at[m, 2, k - 1], s_recv.at[m, 2, k - 1], along(1, k)[1]))
        return early, late

    def gather_pass(m, early, late):
        for part in range(3):
            axis = ORDERS[part][2]
            early[part][0].wait_recv()
            late.append(gather_step(m, part, along(axis, 3)[0], 0, 1, 4))
            early[part][1].wait_recv()
            late.append(gather_step(m, part, along(axis, 1)[0], 1, 3, 5))

    def feed(m):
        total = jnp.sum(stats[m].reshape(16, N, 8, 128), axis=0)
        columns = []
        for zz in range(N):
            spread = jnp.transpose(jnp.broadcast_to(total[zz, 0:1], (128, 128)))
            columns.append(spread[0:32])
        row_scale = lax.rsqrt(jnp.concatenate(columns, axis=0) * (1.0 / 8192) + EPS)
        row_scale = jnp.concatenate([row_scale, row_scale], axis=1)
        features = jnp.concatenate(
            [gathered[m, i, j].reshape(128, 512) for i in range(N) for j in range(N)], axis=1
        )
        for p in range(2):
            gate = dot(features, w_all[p, :, 0:256]) * row_scale
            up = dot(features, w_all[p, :, 256:512]) * row_scale
            hid[m, core, :, p * 256:(p + 1) * 256] = (gate / (1.0 + jnp.exp(-gate)) * up).astype(BF16)
        block = hid.at[m, core]
        return remote(block, block, sib_send.at[12 + m], sib_recv.at[12 + m], sibling)

    def residual(m):
        row = pl.multiple_of(xy * 8, 8)
        wanted = jnp.concatenate([pick[m, 0, pl.ds(row, 8), :], pick[m, 2, pl.ds(row, 8), :]], axis=0).astype(BF16)
        found = [dot(wanted, gathered[m, shard, j].reshape(128, 512)) for j in range(N)]
        found = jnp.concatenate(found, axis=1)
        res_own[m] = found[0:8]
        res_send[m] = jnp.concatenate([found[8:16, 0:1024], found[8:16, 1024:2048]], axis=0).astype(BF16)
        return remote(res_send.at[m], res_recv.at[m], sib_send.at[14 + m], sib_recv.at[14 + m], sibling)

    sums = (sums0, sums1, sums2)
    via = (via0, via1, via2)
    in1 = (in10, in11, in12)
    t1 = (t10, t11, t12)
    in2 = (in20, in21, in22)
    t2 = (t20, t21, t22)
    in3 = (in30, in31, in32)

    def sum_index(part, coord, half):
        axis = ORDERS[part][0]
        index = [slice(None)] * 3
        index[1 if axis == 0 else 0] = pl.ds(half * 2, 2)
        index[axis] = coord
        return index

    def reduce_step(m, part, coord, half, dst, k, slot):
        index = sum_index(part, coord, half)
        return remote(
            sums[part].at[m, index[0], index[1], index[2]], dst,
            r_send.at[m, 0, part, slot], r_recv.at[m, 0, part, slot], along(ORDERS[part][0], k)[1],
        )

    def down(m):
        other = jnp.where(core == 0, hid[m, 1].astype(F32), hid[m, 0].astype(F32)).astype(BF16)
        ours = dot(pick[m, 0].astype(BF16), hid[m, core]) + dot(pick[m, 1].astype(BF16), other)
        ours = ours.astype(BF16)
        copies = [[], [], []]
        for part in range(3):
            width = COLS[part]
            for zz in range(N):
                base = ((zz % 2) * 2 + zz // 2) * 2048 + STARTS[part]
                halves = []
                for half in range(2):
                    lanes = pl.ds(base + half * 1024, width)
                    value = dot(ours[:, 0:256], wd_all[0, :, lanes]) + dot(ours[:, 256:512], wd_all[1, :, lanes])
                    halves.append(value.reshape(16, 1, 8, width))
                both = jnp.concatenate(halves, axis=1).reshape(N, N, 16, width)
                sums[part][m, :, :, zz] = both.astype(BF16)
            far = along(ORDERS[part][0], 2)[0]
            ahead, back = along(ORDERS[part][0], 1)[0], along(ORDERS[part][0], 3)[0]
            copies[part] = [
                reduce_step(m, part, far, 0, via[part].at[m, 0], 1, 0),
                reduce_step(m, part, far, 1, via[part].at[m, 1], 3, 1),
                reduce_step(m, part, ahead, 1, in1[part].at[m, 0, pl.ds(2, 2)], 1, 2),
                reduce_step(m, part, back, 0, in1[part].at[m, 1, pl.ds(0, 2)], 3, 3),
            ]
        return copies

    def reduce_pass(m, copies):
        for part in range(3):
            for half, k in ((0, 1), (1, 3)):
                there = along(ORDERS[part][0], k)[0]
                copies[part][half].wait_recv()
                index = sum_index(part, there, half)
                own = sums[part][m, index[0], index[1], index[2]].astype(F32)
                sums[part][m, index[0], index[1], index[2]] = (own + via[part][m, half].astype(F32)).astype(BF16)
                copies[part].append(reduce_step(
                    m, part, there, half, in1[part].at[m, half, pl.ds(half * 2, 2)], k, 4 + half
                ))

    def add(own, incoming):
        total = own.astype(F32)
        for term in incoming:
            total = total + term.astype(F32)
        return total

    def reduce_second(m, copies):
        started = [[], [], []]
        for part in range(3):
            received(copies[part][2:])
            axes = ORDERS[part]
            for i in range(N):
                if axes[0] == 0:
                    own = sums[part][m, x, i]
                elif axes[0] == 1:
                    own = sums[part][m, i, y]
                else:
                    own = sums[part][m, i, :, z]
                t1[part][m, i] = add(own, [in1[part][m, q, i] for q in range(2)]).astype(BF16)
            first = axes[1] < axes[2]
            for k in (1, 2, 3):
                there, target = along(axes[1], k)
                src = t1[part].at[m, there] if first else t1[part].at[m, :, there]
                started[part].append(remote(
                    src, in2[part].at[m, k - 1],
                    r_send.at[m, 1, part, k - 1], r_recv.at[m, 1, part, k - 1], target,
                ))
        return started

    def reduce_third(m, copies):
        started = [[], [], []]
        for part in range(3):
            received(copies[part])
            axes = ORDERS[part]
            coord = here[axes[1]]
            own = t1[part][m, coord] if axes[1] < axes[2] else t1[part][m, :, coord]
            t2[part][m] = add(own, [in2[part][m, q] for q in range(3)]).astype(BF16)
            for k in (1, 2, 3):
                there, target = along(axes[2], k)
                started[part].append(remote(
                    t2[part].at[m, there], in3[part].at[m, k - 1],
                    r_send.at[m, 2, part, k - 1], r_recv.at[m, 2, part, k - 1], target,
                ))
        return started

    def finish(m, copies, res_copy):
        received([res_copy])
        pieces = [stats[m, shard, j, z, 4 + q:5 + q] for j in range(N) for q in range(4)]
        across = res_recv[m].astype(F32)
        across = jnp.concatenate([across[0:8], across[8:16]], axis=1)
        base = (res_own[m] + across) / jnp.concatenate(pieces, axis=1)
        for part in range(3):
            received(copies[part])
            own = t2[part][m, here[ORDERS[part][2]]]
            total = add(own, [in3[part][m, q] for q in range(3)])
            for half in range(2):
                start = half * 1024 + STARTS[part]
                lanes = slice(start, start + COLS[part])
                out_ref[m, :, lanes] = (base[:, lanes] + total[half * 8:half * 8 + 8]).astype(BF16)

    attend(0)
    attend(1)
    gain_load.wait()
    gain_all[core, 0:2] = gain_ref[...]
    gain_all[core, 2:8] = jnp.zeros((6, 128), F32)
    pl.semaphore_wait(barrier, 10)
    a0 = attended_phase(0, 0)
    a1 = attended_phase(1, 0)
    wo_copy = remote(wo_ref, wo_all.at[core], sib_send.at[0], sib_recv.at[0], sibling)
    resid_copy = remote(resid_ref, resid_all.at[core], sib_send.at[1], sib_recv.at[1], sibling)
    gain_copy = remote(gain_all.at[core], gain_all.at[core], sib_send.at[2], sib_recv.at[2], sibling)
    wd_load = local(wd_ref, wd_all.at[core], local_sem.at[6])
    for chunk in range(0, 2):
        untangle(chunk)
        share(chunk)
    received(a0)
    a0 = attended_phase(0, 1)
    received(a1)
    a1 = attended_phase(1, 1)
    wd_copy = remote(wd_ref, wd_all.at[core], sib_send.at[3], sib_recv.at[3], sibling)
    rows_load.wait()
    choose(0)
    choose(1)
    for chunk in range(2, 4):
        untangle(chunk)
        share(chunk)
    other_loads["wo"].wait()
    wo_copy.wait_recv()
    other_loads["resid"].wait()
    resid_copy.wait_recv()
    gain_copy.wait_recv()
    received(a0)
    b0 = project(0)
    gain_row = jnp.concatenate(
        [gain_all[0, 0:1], gain_all[0, 1:2], gain_all[1, 0:1], gain_all[1, 1:2]], axis=1
    )
    resid0 = residual_rows(0)
    resid1 = residual_rows(1)
    untangle(4)
    share(4)
    received(a1)
    b1 = project(1)
    untangle(5)
    share(5)
    received(b0)
    mix(0, resid0, gain_row)
    g0 = gather_phase(0, 0)
    received(b1)
    mix(1, resid1, gain_row)
    g1 = gather_phase(1, 0)
    for chunk in range(6, W_CHUNKS):
        untangle(chunk)
        share(chunk)
    received(g0)
    g0 = gather_phase(0, 1)
    received(g1)
    g1 = gather_phase(1, 1)
    received(g0)
    early = len(all_sends)
    g0, l0 = gather_last(0)
    received(g1)
    gather_pass(0, g0, l0)
    g1, l1 = gather_last(1)
    gather_pass(1, g1, l1)
    drain(early)
    early = len(all_sends)
    received(weight_copies.values())
    received(l0)
    h0 = feed(0)
    wd_load.wait()
    wd_copy.wait_recv()
    received([h0])
    r0 = down(0)
    c0 = residual(0)
    received(l1)
    h1 = feed(1)
    reduce_pass(0, r0)
    received([h1])
    middle = len(all_sends)
    r1 = down(1)
    c1 = residual(1)
    drain(early)
    middle = middle - early
    r0 = reduce_second(0, r0)
    reduce_pass(1, r1)
    r0 = reduce_third(0, r0)
    r1 = reduce_second(1, r1)
    drain(middle)
    early = len(all_sends)
    finish(0, r0, c0)
    r1 = reduce_third(1, r1)
    drain(early - 9)
    finish(1, r1, c1)

    for copy in all_sends:
        copy.wait_send()


def shards(query, cache, cache_len, row_slot, resid, w_out, norm_gain, w_gate_up, w_down):
    raw = w_gate_up.reshape(8192, 2, 2, 128).transpose(0, 2, 1, 3).reshape(32768, 128)
    vmem = pl.BlockSpec(memory_space=pltpu.VMEM)
    smem = pl.BlockSpec(memory_space=pltpu.SMEM)
    hbm = pl.BlockSpec(memory_space=pl.ANY)
    sem = pltpu.SemaphoreType.DMA
    scratch = [
        pltpu.VMEM((MICRO, 8, 2048), BF16),
        pltpu.VMEM((MICRO, 256), jnp.int32),
        pltpu.VMEM((2, 128), F32),
        pltpu.VMEM((MICRO, 2, 8, 1024, 128), BF16),
        pltpu.VMEM((MICRO, N, N, 16, 1024), BF16),
        pltpu.VMEM((2, 2048, 256), BF16),
        pltpu.VMEM((2, 512, 256), BF16),
        pltpu.VMEM((2, 8, 128), F32),
        pltpu.VMEM((W_SLOTS, 32768 // W_CHUNKS, 128), BF16),
        pltpu.VMEM((2, 8192, 512), BF16),
        pltpu.VMEM((2, 256, 8192), BF16),
        pltpu.VMEM((MICRO, N, 32, 512), BF16),
        pltpu.VMEM((MICRO, 3, 32, 512), BF16),
        pltpu.VMEM((MICRO, N, N, N, 32, 512), BF16),
        pltpu.VMEM((MICRO, N, N, N, 8, 128), F32),
        pltpu.VMEM((MICRO, 2, 128, 512), BF16),
        pltpu.VMEM((MICRO, 3, 128, 128), F32),
    ]
    scratch += [pltpu.VMEM((MICRO, N, N, N, 16, c), BF16) for c in COLS]
    scratch += [pltpu.VMEM((MICRO, 2, 2, N, 16, c), BF16) for c in COLS]
    scratch += [pltpu.VMEM((MICRO, 2, N, N, 16, c), BF16) for c in COLS]
    scratch += [pltpu.VMEM((MICRO, N, N, 16, c), BF16) for c in COLS]
    scratch += [pltpu.VMEM((MICRO, 3, N, 16, c), BF16) for c in COLS]
    scratch += [pltpu.VMEM((MICRO, N, 16, c), BF16) for c in COLS]
    scratch += [pltpu.VMEM((MICRO, 3, 16, c), BF16) for c in COLS]
    scratch += [
        pltpu.VMEM((MICRO, 8, 2048), F32),
        pltpu.VMEM((MICRO, 16, 1024), BF16),
        pltpu.VMEM((MICRO, 16, 1024), BF16),
    ]
    scratch += [
        sem((10 + W_CHUNKS,)),
        sem((16,)), sem((16,)),
        sem((MICRO, 2, 2, 3)), sem((MICRO, 2, 2, 3)),
        sem((MICRO, 3)), sem((MICRO, 3)),
        sem((MICRO, 3, 3, 6)), sem((MICRO, 3, 3, 6)),
        sem((MICRO, 3, 3)), sem((MICRO, 3, 3)),
        sem((MICRO, 3, 3, 6)), sem((MICRO, 3, 3, 6)),
    ]
    return pl.pallas_call(
        layer_kernel,
        out_shape=jax.ShapeDtypeStruct((MICRO, 8, 2048), BF16),
        in_specs=[smem] + [hbm] * 8,
        out_specs=vmem,
        scratch_shapes=scratch,
        compiler_params=pltpu.CompilerParams(
            collective_id=0, has_side_effects=True, vmem_limit_bytes=62 * 1024 * 1024
        ),
        name="layer",
    )(
        cache_len, query, cache.reshape(MICRO, 8, 2, 1024, 128), row_slot, resid.reshape(512, 256), w_out,
        norm_gain.reshape(2, 128), raw, w_down,
    )


def solution(mesh):
    placed = (
        P(None, "grp", ("side", "tp")),
        P(None, "grp", None, ("side", "tp"), None, None),
        P(None, "grp"),
        P(),
        P(None, None, "grp"),
        P(("side", "tp"), "grp"),
        P("grp"),
        P(None, None, ("side", "grp", "tp")),
        P(("side", "grp", "tp"), None),
    )
    return jax.shard_map(
        shards,
        mesh=mesh,
        in_specs=placed,
        out_specs=P(None, "grp", ("side", "tp")),
        check_vma=False,
    )
```

```python
import math

import jax
import jax.numpy as jnp
from jax import lax
from jax.experimental import pallas as pl
from jax.experimental.pallas import tpu as pltpu
from jax.sharding import PartitionSpec as P

MESH = pl.DeviceIdType.MESH
F32 = jnp.float32
BF16 = jnp.bfloat16
EPS = 1e-05
N = 4
MICRO = 2
COLS = (384, 384, 256)
STARTS = (0, 384, 768)
GATHER_PARTS = ((0, 16, 0, 384), (16, 16, 0, 384), (0, 32, 384, 128))
ORDERS = ((0, 1, 2), (1, 2, 0), (2, 0, 1))
W_CHUNKS = 8
W_SLOTS = 3


def dot(a, b):
    return jnp.dot(a, b, preferred_element_type=F32)


def layer_kernel(
    len_ref, query_ref, cache_ref, rows_in, resid_ref, wo_ref, gain_in, wg_ref, wd_ref,
    out_ref,
    rows_ref, gain_ref, kv, att_all, wo_all, resid_all, gain_all, w_raw, w_all, wd_all,
    proj_send, proj_recv, gathered, stats, hid, pick,
    sums0, sums1, sums2, via0, via1, via2, in10, in11, in12, t10, t11, t12,
    in20, in21, in22, t20, t21, t22, in30, in31, in32,
    res_own, res_send, res_recv,
    local_sem, sib_send, sib_recv, a_send, a_recv, b_send, b_recv,
    g_send, g_recv, s_send, s_recv, r_send, r_recv,
):
    g = lax.axis_index("grp")
    side = lax.axis_index("side")
    tp = lax.axis_index("tp")
    core = lax.rem(g, 2)
    y = lax.rem(g // 2, N)
    x = g // 8
    z = tp * 2 + side
    here = (x, y, z)
    xy = x * N + y
    shard = side * 2 + tp

    def device(cx, cy, cz, cc):
        return {"side": lax.rem(cz, 2), "grp": (cx * N + cy) * 2 + cc, "tp": cz // 2}

    def along(axis, k):
        moved = list(here)
        moved[axis] = lax.rem(here[axis] + k, N)
        return moved[axis], device(moved[0], moved[1], moved[2], core)

    sibling = device(x, y, z, 1 - core)
    all_sends = []

    def remote(src, dst, send, recv, target):
        copy = pltpu.make_async_remote_copy(
            src_ref=src, dst_ref=dst, send_sem=send, recv_sem=recv,
            device_id=target, device_id_type=MESH,
        )
        copy.start()
        all_sends.append(copy)
        return copy

    def local(src, dst, sem):
        copy = pltpu.make_async_copy(src, dst, sem)
        copy.start()
        return copy

    def drain(count):
        for copy in all_sends[:count]:
            copy.wait_send()
        del all_sends[:count]

    def received(copies):
        for copy in copies:
            copy.wait_recv()

    barrier = pltpu.get_barrier_semaphore()
    for axis in range(3):
        for k in (1, 2, 3):
            pl.semaphore_signal(barrier, inc=1, device_id=along(axis, k)[1], device_id_type=MESH)
    pl.semaphore_signal(barrier, inc=1, device_id=sibling, device_id_type=MESH)

    def load_kv(m):
        return [local(cache_ref.at[m, :, i], kv.at[m, i], local_sem.at[m * 2 + i]) for i in range(2)]

    kv_loads = {0: load_kv(0), 1: load_kv(1)}
    rows_load = local(rows_in, rows_ref, local_sem.at[7])
    gain_load = local(gain_in, gain_ref, local_sem.at[9 + W_CHUNKS])
    raw_rows = w_raw.shape[1]

    def load_raw(chunk):
        return local(
            wg_ref.at[pl.ds(chunk * raw_rows, raw_rows)], w_raw.at[chunk % W_SLOTS], local_sem.at[8 + chunk]
        )

    raw_loads = {}
    other_loads = {}

    def load_rest():
        other_loads["wo"] = local(wo_ref, wo_all.at[core], local_sem.at[4])
        other_loads["resid"] = local(resid_ref, resid_all.at[core], local_sem.at[5])
        for chunk in range(W_SLOTS):
            raw_loads[chunk] = load_raw(chunk)

    def attend(m):
        queries = query_ref[m].astype(F32)
        heads = queries.shape[1] // 128
        stacked = jnp.concatenate([queries[:, h * 128:(h + 1) * 128] for h in range(heads)], axis=0).astype(BF16)
        slot_id = lax.broadcasted_iota(jnp.int32, (heads * 8, 1), 0) % 8
        live = jnp.zeros((heads * 8, 1), jnp.int32)
        for s in range(8):
            live = jnp.where(slot_id == s, len_ref[m, s], live)
        kv_loads[m][0].wait()
        if m == 0:
            load_rest()
        scores = None
        for s in range(8):
            one = lax.dot_general(stacked, kv[m, 0, s], (((1,), (1,)), ((), ())), preferred_element_type=F32)
            scores = one if s == 0 else jnp.where(slot_id == s, one, scores)
        position = lax.broadcasted_iota(jnp.int32, scores.shape, 1)
        scores = jnp.where(position < live, scores * (1.0 / math.sqrt(128)), -jnp.inf)
        top = jnp.max(scores, axis=1, keepdims=True)
        raised = jnp.exp(scores - top)
        total = jnp.sum(raised, axis=1, keepdims=True)
        weights = (raised / total).astype(BF16)
        kv_loads[m][1].wait()
        mixed = None
        for s in range(8):
            one = dot(weights, kv[m, 1, s])
            mixed = one if s == 0 else jnp.where(slot_id == s, one, mixed)
        halves = []
        for half in range(2):
            tiles = [mixed[(half * 8 + h) * 8:(half * 8 + h) * 8 + 8] for h in range(8)]
            halves.append(jnp.concatenate(tiles, axis=1))
        att_all[m, x, y] = jnp.concatenate(halves, axis=0).astype(BF16)

    def attended_phase(m, phase):
        copies = []
        for part in range(2):
            cols = pl.ds(part * 512, 512)
            axis = part if phase == 0 else 1 - part
            index = [x, y]
            if phase == 1:
                index[part] = slice(None)
            ref = att_all.at[m, index[0], index[1], :, cols]
            for k in (1, 2, 3):
                copies.append(remote(
                    ref, ref, a_send.at[m, phase, part, k - 1], a_recv.at[m, phase, part, k - 1], along(axis, k)[1]
                ))
        return copies

    p_out = lax.broadcasted_iota(jnp.int32, (256, 256), 0)
    p_in = lax.broadcasted_iota(jnp.int32, (256, 256), 1)
    order = jnp.where(p_in == (p_out % 64) * 4 + p_out // 64, 1.0, 0.0).astype(BF16)
    weight_copies = {}

    def untangle(chunk):
        raw_loads[chunk].wait()
        slot = chunk % W_SLOTS

        tiles = raw_rows // 256
        mixed = jnp.concatenate([w_raw[slot, q * 256:(q + 1) * 256] for q in range(tiles)], axis=1)
        apart = dot(order, mixed)
        for l in range(2):
            for c in range(2):
                rows = slice((l * 2 + c) * 64, (l * 2 + c) * 64 + 64)
                lanes = pl.ds(c * 256 + l * 128, 128)
                for q in range(tiles):
                    base = (chunk * tiles + q) * 64
                    w_all[core, pl.ds(base, 64), lanes] = apart[rows, q * 128:(q + 1) * 128].astype(BF16)
        if chunk + W_SLOTS < W_CHUNKS:
            raw_loads[chunk + W_SLOTS] = load_raw(chunk + W_SLOTS)

    def share(chunk):
        span = raw_rows // 512
        block = w_all.at[core, pl.ds(chunk * span * 128, span * 128)]
        weight_copies[chunk] = remote(block, block, sib_send.at[4 + chunk], sib_recv.at[4 + chunk], sibling)

    def slot_of(r, parity):
        return ((r // 8) * 2 + parity) * 8 + r % 8

    def choose(m):
        r = lax.broadcasted_iota(jnp.int32, (128, 256), 0)
        for i, parity in enumerate((core, 1 - core)):
            hit = jnp.where(slot_of(r, parity) == rows_ref[m:m + 1, :], 1.0, 0.0)
            turned = jnp.concatenate([jnp.transpose(hit[:, 0:128]), jnp.transpose(hit[:, 128:256])], axis=0)
            turned = turned.reshape(16, 2, 8, 128)
            even, odd = turned[:, 0].reshape(128, 128), turned[:, 1].reshape(128, 128)
            pick[m, i] = jnp.where(core == 0, even, odd)
            if i == 0:
                pick[m, 2] = jnp.where(core == 0, odd, even)

    def project(m):
        blocks = att_all[m].astype(F32).reshape(16, 2, 8, 1024)
        rows = jnp.concatenate([blocks[:, 0].reshape(128, 1024), blocks[:, 1].reshape(128, 1024)], axis=1).astype(BF16)
        for c in range(2):
            proj_send[m, :, :, c * 256:(c + 1) * 256] = dot(rows, wo_all[c]).astype(BF16).reshape(N, 32, 256)
        copies = []
        for k in (1, 2, 3):
            there, target = along(2, k)
            copies.append(remote(
                proj_send.at[m, there], proj_recv.at[m, k - 1], b_send.at[m, k - 1], b_recv.at[m, k - 1], target
            ))
        return copies

    def residual_rows(m):
        r = z * 32 + lax.broadcasted_iota(jnp.int32, (32, 256), 0)
        served = jnp.where(slot_of(r, core) == rows_ref[m:m + 1, :], 1.0, 0.0).astype(BF16)
        return jnp.concatenate([dot(served, resid_all[c, m * 256:(m + 1) * 256]) for c in range(2)], axis=1)

    def mix(m, resid_rows, gain_row):
        mixed = resid_rows + (
            (proj_send[m, z].astype(F32) + proj_recv[m, 0].astype(F32))
            + (proj_recv[m, 1].astype(F32) + proj_recv[m, 2].astype(F32))
        )
        gathered[m, x, y, z] = (mixed * gain_row).astype(BF16)
        squares = jnp.sum(mixed * mixed, axis=1, keepdims=True)
        tall = jnp.concatenate([jnp.broadcast_to(squares, (32, 128)), jnp.zeros((96, 128), F32)], axis=0)
        stats[m, x, y, z, 0:4] = jnp.transpose(tall)[0:4]
        stats[m, x, y, z, 4:6] = gain_all[0, 0:2]
        stats[m, x, y, z, 6:8] = gain_all[1, 0:2]

    def gather_phase(m, phase):
        copies = []
        for part, (row, rows, col, cols) in enumerate(GATHER_PARTS):
            axes = ORDERS[part]
            index = list(here)
            for done in axes[:phase]:
                index[done] = slice(None)
            block = gathered.at[m, index[0], index[1], index[2], pl.ds(row, rows), pl.ds(col, cols)]
            for k in (1, 2, 3):
                target = along(axes[phase], k)[1]
                copies.append(remote(
                    block, block, g_send.at[m, phase, part, k - 1], g_recv.at[m, phase, part, k - 1], target
                ))
                if part == 2:
                    tile = stats.at[m, index[0], index[1], index[2]]
                    copies.append(remote(
                        tile, tile, s_send.at[m, phase, k - 1], s_recv.at[m, phase, k - 1], target
                    ))
        return copies

    def gather_block(m, part, coord, half):
        axis = ORDERS[part][2]
        row, rows, col, cols = GATHER_PARTS[part]
        index = [slice(None)] * 3
        index[min(ORDERS[part][:2])] = pl.ds(half * 2, 2)
        index[axis] = coord
        return gathered.at[m, index[0], index[1], index[2], pl.ds(row, rows), pl.ds(col, cols)]

    def gather_step(m, part, coord, half, k, slot):
        block = gather_block(m, part, coord, half)
        return remote(
            block, block, g_send.at[m, 2, part, slot], g_recv.at[m, 2, part, slot], along(ORDERS[part][2], k)[1]
        )

    def gather_last(m):
        own = [here[ORDERS[part][2]] for part in range(3)]
        early = [
            (gather_step(m, part, own[part], 0, 1, 0), gather_step(m, part, own[part], 1, 3, 1)) for part in range(3)
        ]
        late = []
        for part in range(3):
            late.append(gather_step(m, part, own[part], 1, 1, 2))
            late.append(gather_step(m, part, own[part], 0, 3, 3))
        for k in (1, 2, 3):
            tile = stats.at[m, :, y]
            late.append(remote(tile, tile, s_send.at[m, 2, k - 1], s_recv.at[m, 2, k - 1], along(1, k)[1]))
        return early, late

    def gather_pass(m, early, late):
        for part in range(3):
            axis = ORDERS[part][2]
            early[part][0].wait_recv()
            late.append(gather_step(m, part, along(axis, 3)[0], 0, 1, 4))
            early[part][1].wait_recv()
            late.append(gather_step(m, part, along(axis, 1)[0], 1, 3, 5))

    def feed(m):
        total = jnp.sum(stats[m].reshape(16, N, 8, 128), axis=0)
        columns = []
        for zz in range(N):
            spread = jnp.transpose(jnp.broadcast_to(total[zz, 0:1], (128, 128)))
            columns.append(spread[0:32])
        row_scale = lax.rsqrt(jnp.concatenate(columns, axis=0) * (1.0 / 8192) + EPS)
        row_scale = jnp.concatenate([row_scale, row_scale], axis=1)
        features = jnp.concatenate(
            [gathered[m, i, j].reshape(128, 512) for i in range(N) for j in range(N)], axis=1
        )
        for p in range(2):
            gate = dot(features, w_all[p, :, 0:256]) * row_scale
            up = dot(features, w_all[p, :, 256:512]) * row_scale
            hid[m, core, :, p * 256:(p + 1) * 256] = (gate / (1.0 + jnp.exp(-gate)) * up).astype(BF16)
        block = hid.at[m, core]
        return remote(block, block, sib_send.at[12 + m], sib_recv.at[12 + m], sibling)

    def residual(m):
        row = pl.multiple_of(xy * 8, 8)
        wanted = jnp.concatenate([pick[m, 0, pl.ds(row, 8), :], pick[m, 2, pl.ds(row, 8), :]], axis=0).astype(BF16)
        found = [dot(wanted, gathered[m, shard, j].reshape(128, 512)) for j in range(N)]
        found = jnp.concatenate(found, axis=1)
        res_own[m] = found[0:8]
        res_send[m] = jnp.concatenate([found[8:16, 0:1024], found[8:16, 1024:2048]], axis=0).astype(BF16)
        return remote(res_send.at[m], res_recv.at[m], sib_send.at[14 + m], sib_recv.at[14 + m], sibling)

    sums = (sums0, sums1, sums2)
    via = (via0, via1, via2)
    in1 = (in10, in11, in12)
    t1 = (t10, t11, t12)
    in2 = (in20, in21, in22)
    t2 = (t20, t21, t22)
    in3 = (in30, in31, in32)

    def sum_index(part, coord, half):
        axis = ORDERS[part][0]
        index = [slice(None)] * 3
        index[1 if axis == 0 else 0] = pl.ds(half * 2, 2)
        index[axis] = coord
        return index

    def reduce_step(m, part, coord, half, dst, k, slot):
        index = sum_index(part, coord, half)
        return remote(
            sums[part].at[m, index[0], index[1], index[2]], dst,
            r_send.at[m, 0, part, slot], r_recv.at[m, 0, part, slot], along(ORDERS[part][0], k)[1],
        )

    def down(m):
        other = jnp.where(core == 0, hid[m, 1].astype(F32), hid[m, 0].astype(F32)).astype(BF16)
        ours = dot(pick[m, 0].astype(BF16), hid[m, core]) + dot(pick[m, 1].astype(BF16), other)
        ours = ours.astype(BF16)
        copies = [[], [], []]
        for part in range(3):
            width = COLS[part]
            for zz in range(N):
                base = ((zz % 2) * 2 + zz // 2) * 2048 + STARTS[part]
                halves = []
                for half in range(2):
                    lanes = pl.ds(base + half * 1024, width)
                    value = dot(ours[:, 0:256], wd_all[0, :, lanes]) + dot(ours[:, 256:512], wd_all[1, :, lanes])
                    halves.append(value.reshape(16, 1, 8, width))
                both = jnp.concatenate(halves, axis=1).reshape(N, N, 16, width)
                sums[part][m, :, :, zz] = both.astype(BF16)
            far = along(ORDERS[part][0], 2)[0]
            ahead, back = along(ORDERS[part][0], 1)[0], along(ORDERS[part][0], 3)[0]
            copies[part] = [
                reduce_step(m, part, far, 0, via[part].at[m, 0], 1, 0),
                reduce_step(m, part, far, 1, via[part].at[m, 1], 3, 1),
                reduce_step(m, part, ahead, 1, in1[part].at[m, 0, pl.ds(2, 2)], 1, 2),
                reduce_step(m, part, back, 0, in1[part].at[m, 1, pl.ds(0, 2)], 3, 3),
            ]
        return copies

    def reduce_pass(m, copies):
        for part in range(3):
            for half, k in ((0, 1), (1, 3)):
                there = along(ORDERS[part][0], k)[0]
                copies[part][half].wait_recv()
                index = sum_index(part, there, half)
                own = sums[part][m, index[0], index[1], index[2]].astype(F32)
                sums[part][m, index[0], index[1], index[2]] = (own + via[part][m, half].astype(F32)).astype(BF16)
                copies[part].append(reduce_step(
                    m, part, there, half, in1[part].at[m, half, pl.ds(half * 2, 2)], k, 4 + half
                ))

    def add(own, incoming):
        total = own.astype(F32)
        for term in incoming:
            total = total + term.astype(F32)
        return total

    def reduce_second(m, copies):
        started = [[], [], []]
        for part in range(3):
            received(copies[part][2:])
            axes = ORDERS[part]
            for i in range(N):
                if axes[0] == 0:
                    own = sums[part][m, x, i]
                elif axes[0] == 1:
                    own = sums[part][m, i, y]
                else:
                    own = sums[part][m, i, :, z]
                t1[part][m, i] = add(own, [in1[part][m, q, i] for q in range(2)]).astype(BF16)
            first = axes[1] < axes[2]
            for k in (1, 2, 3):
                there, target = along(axes[1], k)
                src = t1[part].at[m, there] if first else t1[part].at[m, :, there]
                started[part].append(remote(
                    src, in2[part].at[m, k - 1],
                    r_send.at[m, 1, part, k - 1], r_recv.at[m, 1, part, k - 1], target,
                ))
        return started

    def reduce_third(m, copies):
        started = [[], [], []]
        for part in range(3):
            received(copies[part])
            axes = ORDERS[part]
            coord = here[axes[1]]
            own = t1[part][m, coord] if axes[1] < axes[2] else t1[part][m, :, coord]
            t2[part][m] = add(own, [in2[part][m, q] for q in range(3)]).astype(BF16)
            for k in (1, 2, 3):
                there, target = along(axes[2], k)
                started[part].append(remote(
                    t2[part].at[m, there], in3[part].at[m, k - 1],
                    r_send.at[m, 2, part, k - 1], r_recv.at[m, 2, part, k - 1], target,
                ))
        return started

    def finish(m, copies, res_copy):
        received([res_copy])
        pieces = [stats[m, shard, j, z, 4 + q:5 + q] for j in range(N) for q in range(4)]
        across = res_recv[m].astype(F32)
        across = jnp.concatenate([across[0:8], across[8:16]], axis=1)
        base = (res_own[m] + across) / jnp.concatenate(pieces, axis=1)
        for part in range(3):
            received(copies[part])
            own = t2[part][m, here[ORDERS[part][2]]]
            total = add(own, [in3[part][m, q] for q in range(3)])
            for half in range(2):
                start = half * 1024 + STARTS[part]
                lanes = slice(start, start + COLS[part])
                out_ref[m, :, lanes] = (base[:, lanes] + total[half * 8:half * 8 + 8]).astype(BF16)

    attend(0)
    attend(1)
    gain_load.wait()
    gain_all[core, 0:2] = gain_ref[...]
    gain_all[core, 2:8] = jnp.zeros((6, 128), F32)
    pl.semaphore_wait(barrier, 10)
    a0 = attended_phase(0, 0)
    a1 = attended_phase(1, 0)
    wo_copy = remote(wo_ref, wo_all.at[core], sib_send.at[0], sib_recv.at[0], sibling)
    resid_copy = remote(resid_ref, resid_all.at[core], sib_send.at[1], sib_recv.at[1], sibling)
    gain_copy = remote(gain_all.at[core], gain_all.at[core], sib_send.at[2], sib_recv.at[2], sibling)
    wd_load = local(wd_ref, wd_all.at[core], local_sem.at[6])
    for chunk in range(0, 2):
        untangle(chunk)
        share(chunk)
    received(a0)
    a0 = attended_phase(0, 1)
    received(a1)
    a1 = attended_phase(1, 1)
    wd_copy = remote(wd_ref, wd_all.at[core], sib_send.at[3], sib_recv.at[3], sibling)
    rows_load.wait()
    choose(0)
    choose(1)
    for chunk in range(2, 4):
        untangle(chunk)
        share(chunk)
    other_loads["wo"].wait()
    wo_copy.wait_recv()
    other_loads["resid"].wait()
    resid_copy.wait_recv()
    gain_copy.wait_recv()
    received(a0)
    b0 = project(0)
    gain_row = jnp.concatenate(
        [gain_all[0, 0:1], gain_all[0, 1:2], gain_all[1, 0:1], gain_all[1, 1:2]], axis=1
    )
    resid0 = residual_rows(0)
    resid1 = residual_rows(1)
    untangle(4)
    share(4)
    received(a1)
    b1 = project(1)
    untangle(5)
    share(5)
    received(b0)
    mix(0, resid0, gain_row)
    g0 = gather_phase(0, 0)
    received(b1)
    mix(1, resid1, gain_row)
    g1 = gather_phase(1, 0)
    for chunk in range(6, W_CHUNKS):
        untangle(chunk)
        share(chunk)
    received(g0)
    g0 = gather_phase(0, 1)
    received(g1)
    g1 = gather_phase(1, 1)
    received(g0)
    early = len(all_sends)
    g0, l0 = gather_last(0)
    received(g1)
    gather_pass(0, g0, l0)
    g1, l1 = gather_last(1)
    gather_pass(1, g1, l1)
    drain(early)
    early = len(all_sends)
    received(weight_copies.values())
    received(l0)
    h0 = feed(0)
    wd_load.wait()
    wd_copy.wait_recv()
    received([h0])
    r0 = down(0)
    c0 = residual(0)
    received(l1)
    h1 = feed(1)
    reduce_pass(0, r0)
    received([h1])
    middle = len(all_sends)
    r1 = down(1)
    drain(early)
    middle = middle - early
    r0 = reduce_second(0, r0)
    reduce_pass(1, r1)
    c1 = residual(1)
    r0 = reduce_third(0, r0)
    r1 = reduce_second(1, r1)
    drain(middle)
    early = len(all_sends)
    finish(0, r0, c0)
    r1 = reduce_third(1, r1)
    drain(early - 9)
    finish(1, r1, c1)

    for copy in all_sends:
        copy.wait_send()


def shards(query, cache, cache_len, row_slot, resid, w_out, norm_gain, w_gate_up, w_down):
    raw = w_gate_up.reshape(8192, 2, 2, 128).transpose(0, 2, 1, 3).reshape(32768, 128)
    vmem = pl.BlockSpec(memory_space=pltpu.VMEM)
    smem = pl.BlockSpec(memory_space=pltpu.SMEM)
    hbm = pl.BlockSpec(memory_space=pl.ANY)
    sem = pltpu.SemaphoreType.DMA
    scratch = [
        pltpu.VMEM((MICRO, 256), jnp.int32),
        pltpu.VMEM((2, 128), F32),
        pltpu.VMEM((MICRO, 2, 8, 1024, 128), BF16),
        pltpu.VMEM((MICRO, N, N, 16, 1024), BF16),
        pltpu.VMEM((2, 2048, 256), BF16),
        pltpu.VMEM((2, 512, 256), BF16),
        pltpu.VMEM((2, 8, 128), F32),
        pltpu.VMEM((W_SLOTS, 32768 // W_CHUNKS, 128), BF16),
        pltpu.VMEM((2, 8192, 512), BF16),
        pltpu.VMEM((2, 256, 8192), BF16),
        pltpu.VMEM((MICRO, N, 32, 512), BF16),
        pltpu.VMEM((MICRO, 3, 32, 512), BF16),
        pltpu.VMEM((MICRO, N, N, N, 32, 512), BF16),
        pltpu.VMEM((MICRO, N, N, N, 8, 128), F32),
        pltpu.VMEM((MICRO, 2, 128, 512), BF16),
        pltpu.VMEM((MICRO, 3, 128, 128), F32),
    ]
    scratch += [pltpu.VMEM((MICRO, N, N, N, 16, c), BF16) for c in COLS]
    scratch += [pltpu.VMEM((MICRO, 2, 2, N, 16, c), BF16) for c in COLS]
    scratch += [pltpu.VMEM((MICRO, 2, N, N, 16, c), BF16) for c in COLS]
    scratch += [pltpu.VMEM((MICRO, N, N, 16, c), BF16) for c in COLS]
    scratch += [pltpu.VMEM((MICRO, 3, N, 16, c), BF16) for c in COLS]
    scratch += [pltpu.VMEM((MICRO, N, 16, c), BF16) for c in COLS]
    scratch += [pltpu.VMEM((MICRO, 3, 16, c), BF16) for c in COLS]
    scratch += [
        pltpu.VMEM((MICRO, 8, 2048), F32),
        pltpu.VMEM((MICRO, 16, 1024), BF16),
        pltpu.VMEM((MICRO, 16, 1024), BF16),
    ]
    scratch += [
        sem((10 + W_CHUNKS,)),
        sem((16,)), sem((16,)),
        sem((MICRO, 2, 2, 3)), sem((MICRO, 2, 2, 3)),
        sem((MICRO, 3)), sem((MICRO, 3)),
        sem((MICRO, 3, 3, 6)), sem((MICRO, 3, 3, 6)),
        sem((MICRO, 3, 3)), sem((MICRO, 3, 3)),
        sem((MICRO, 3, 3, 6)), sem((MICRO, 3, 3, 6)),
    ]
    return pl.pallas_call(
        layer_kernel,
        out_shape=jax.ShapeDtypeStruct((MICRO, 8, 2048), BF16),
        in_specs=[smem, vmem] + [hbm] * 7,
        out_specs=vmem,
        scratch_shapes=scratch,
        compiler_params=pltpu.CompilerParams(
            collective_id=0, has_side_effects=True, vmem_limit_bytes=62 * 1024 * 1024
        ),
        name="layer",
    )(
        cache_len, query, cache.reshape(MICRO, 8, 2, 1024, 128), row_slot, resid.reshape(512, 256), w_out,
        norm_gain.reshape(2, 128), raw, w_down,
    )


def solution(mesh):
    placed = (
        P(None, "grp", ("side", "tp")),
        P(None, "grp", None, ("side", "tp"), None, None),
        P(None, "grp"),
        P(),
        P(None, None, "grp"),
        P(("side", "tp"), "grp"),
        P("grp"),
        P(None, None, ("side", "grp", "tp")),
        P(("side", "grp", "tp"), None),
    )
    return jax.shard_map(
        shards,
        mesh=mesh,
        in_specs=placed,
        out_specs=P(None, "grp", ("side", "tp")),
        check_vma=False,
    )
```
